256 devices in a mesh: noise: 8 (over x, core), region: 32 (over z, y).
Axes of the slice: x: 4, y: 4, z: 8, core: 2. Of those that a mesh axis runs over, the one named last changes fastest.
Arguments:
- target_state: bfloat16 [84, 65536], P(None, 'region'), may hold values from -6 to 6
- noise_field: bfloat16 [8, 84, 65536], P('noise', None, 'region'), may hold values from -6 to 6
- level_index: int32 [8], P('noise'), may hold values from 0 to 19
- send_rows: int32 [32, 32, 128], P('region'), may hold values from 0 to 2047, as said below
- edge_src: int32 [131072], P('region'), may hold values from 0 to 4095, as said below
- edge_dst: int32 [131072], P('region'), may hold values from 0 to 256, as said below
- edge_geom: bfloat16 [4, 131072], P(None, 'region'), may hold values from -1 to 1
- mesh_init: bfloat16 [8192, 512], P('region'), may hold values from -6 to 6
- neighbours: int32 [8192, 32], P('region'), may hold values from 0 to 8191, as said below
- grid_weight: bfloat16 [84, 512], replicated, may hold values from -0.625 to 0.625
- edge_weight: bfloat16 [4, 512], replicated, may hold values from -3 to 3
- message_weight: bfloat16 [512, 512], replicated, may hold values from -0.25 to 0.25
- enc_gain: float32 [512], replicated, may hold values from 0.5 to 1.5
- att_gain: float32 [512], replicated, may hold values from 0.5 to 1.5
- qkv_weight: bfloat16 [512, 1536], replicated, may hold values from -0.25 to 0.25
- out_weight: bfloat16 [512, 512], replicated, may hold values from -0.25 to 0.25
- cotangent: bfloat16 [8, 8192, 512], P('noise', 'region'), may hold values from -0.1875 to 0.1875
Outputs:
- mesh_out: bfloat16 [8, 8192, 512], P('noise', 'region')
- out_grad: float32 [512, 512], replicated
The draws below stay inside these ranges and needn't reach their ends.
Inputs may be any that keep to these rules, and one draw needn't show every extreme that they name: `send_rows`: for band b and region r a leading run of slots, of at least a quarter of 128, holds rows to be sent; the other slots hold 0. In some region every band fills all 128 slots. `edge_src`: only live slots are named: s is below the length of the leading run that band b sends to the edge's region. Padding slots hold 0. In each region the live edge slots come first, a multiple of 128 of them and at least a quarter of 4096; some region fills all of them. The rest are padding with edge_dst 256. `neighbours`: A neighbour of node r * 256 + i has the index r * 256 + i + o modulo 8192, with o between -128 and 128.
All inputs are finite; a program needn't handle non-finite values.
Results may differ from the reference program's by a relative error of at most 0.0065.
Values may be sent and summed in bfloat16 or wider, within the bound.
A program may use at most 64 MiB of HBM per device.

```python
import math
import jax
import jax.numpy as jnp
from jax import lax

D = 512
HEADS = 4
VARS = 84
GEO = 4
PLAN = 20
K_NB = 32
EBLOCK = 128
HALO = 128
M_DEV = 256
G_DEV = 2048
EDGES_DEV = 4096
SLOT = 128
HEAD_DIM = 128
LEVELS = 8
GRID = 65536
MESH = 8192
EDGES = 131072
N_REGION = 32


def slot_counts(key):
    counts_key = jax.random.fold_in(key, 101)
    counts = jax.random.randint(counts_key, (N_REGION, N_REGION), max(SLOT // 4, 1), SLOT + 1)
    full_column = jax.random.randint(jax.random.fold_in(counts_key, 1), (), 0, N_REGION)
    chosen = jnp.arange(N_REGION)[None, :] == full_column
    return jnp.where(chosen, SLOT, counts).astype(jnp.int32)


def live_edges(key):
    live_key = jax.random.fold_in(key, 202)
    block_count = EDGES_DEV // EBLOCK
    live_blocks = jax.random.randint(live_key, (N_REGION,), block_count // 4, block_count + 1)
    busiest = jax.random.randint(jax.random.fold_in(live_key, 1), (), 0, N_REGION)
    region_ids = jnp.arange(N_REGION)
    live_blocks = jnp.where(region_ids == busiest, block_count, live_blocks)
    live_blocks = jnp.where(region_ids == (busiest + 1) % N_REGION, block_count // 4, live_blocks)
    return (live_blocks * EBLOCK).astype(jnp.int32)


def draw_send_rows(key, part):
    counts = slot_counts(key)
    rows_key = jax.random.fold_in(key, 3)
    chosen_rows = jax.random.randint(rows_key, (N_REGION, N_REGION, SLOT), 0, G_DEV)
    chosen_rows = chosen_rows.at[0, 0, 0].set(G_DEV - 1)
    used = jnp.arange(SLOT)[None, None, :] < counts[:, :, None]
    return jnp.where(used, chosen_rows, 0).astype(jnp.int32)


def draw_edge_src(key, part):
    counts = slot_counts(key)
    live = live_edges(key)
    draw_key = jax.random.fold_in(key, 4)
    by_region = counts.T
    ends = jnp.cumsum(by_region, axis=1)
    starts = ends - by_region
    totals = ends[:, -1:]
    picked = jax.random.randint(draw_key, (N_REGION, EDGES_DEV), 0, totals)
    picked = picked.at[:, 0].set(totals[:, 0] - 1)
    source_band = jnp.sum((picked[:, :, None] >= ends[:, None, :]).astype(jnp.int32), axis=2)
    begins = jnp.take_along_axis(starts, source_band, axis=1)
    sources = source_band * SLOT + (picked - begins)
    positions = jnp.arange(EDGES_DEV)[None, :]
    sources = jnp.where(positions < live[:, None], sources, 0)
    return sources.reshape(-1).astype(jnp.int32)


def draw_edge_dst(key, part):
    live = live_edges(key)
    draw_key = jax.random.fold_in(key, 5)
    targets = jax.random.randint(draw_key, (N_REGION, EDGES_DEV), 0, M_DEV)
    targets = targets.at[:, 1].set(0)
    positions = jnp.arange(EDGES_DEV)[None, :]
    targets = jnp.where(positions < live[:, None], targets, M_DEV)
    return targets.reshape(-1).astype(jnp.int32)


def draw_neighbours(key, part):
    draw_key = jax.random.fold_in(key, 6)
    offsets = jax.random.randint(draw_key, (N_REGION, M_DEV, K_NB), -HALO, HALO + 1)
    offsets = offsets.at[:, 0, 0].set(-HALO)
    offsets = offsets.at[:, 0, 1].set(-1)
    offsets = offsets.at[:, 0, 2].set(0)
    offsets = offsets.at[:, M_DEV - 1, K_NB - 1].set(HALO)
    region_ids = jnp.arange(N_REGION)[:, None, None]
    row_ids = jnp.arange(M_DEV)[None, :, None]
    global_ids = (region_ids * M_DEV + row_ids + offsets) % (M_DEV * N_REGION)
    return global_ids.reshape(M_DEV * N_REGION, K_NB).astype(jnp.int32)


def plant(entries, own_key, smallest, high):
    spot = [jax.random.randint(jax.random.fold_in(own_key, axis), (), 0, length) for axis, length in enumerate(entries.shape)]
    widest = entries.shape.index(max(entries.shape))
    neighbour = spot[:widest] + [(spot[widest] + 1) % entries.shape[widest]] + spot[widest + 1:]
    return entries.at[tuple(spot)].set(smallest).at[tuple(neighbour)].set(high)


def levels(rng, dims, cuts, smallest, largest):
    level = 1.0
    for dim, blocks in cuts:
        heights = jax.random.uniform(jax.random.fold_in(jax.random.fold_in(rng, 6), dim), (blocks,), jnp.float32, smallest / len(cuts), largest / len(cuts))
        level = level * jnp.repeat(jnp.exp(heights), dims[dim] // blocks).reshape((-1,) + (1,) * (len(dims) - 1 - dim))
    return level


def bell_draw(key, dims, spread, most, split=(), held_as=jnp.bfloat16):
    level = levels(key, dims, split, -0.22, 0.18) if split else 1.0
    values = jax.random.normal(key, dims, jnp.float32) * spread * level
    return jnp.minimum(jnp.maximum(values, -most), most).astype(held_as)


def setup_inputs(seed: int = 0) -> dict:
    keys = jax.random.split(jax.random.key(seed), 18)
    target_state = bell_draw(keys[0], (VARS, GRID), 1.0, 6.0, ((1, 32),))
    noise_field = bell_draw(keys[1], (LEVELS, VARS, GRID), 1.0, 6.0, ((0, 8), (2, 32)))
    level_index = plant(jax.random.randint(keys[2], (LEVELS,), 0, PLAN), jax.random.fold_in(keys[2], 1), 0, PLAN - 1).astype(jnp.int32)
    send_rows = draw_send_rows(jax.random.fold_in(keys[17], 71), 0)
    edge_src = draw_edge_src(jax.random.fold_in(keys[17], 71), 0)
    edge_dst = draw_edge_dst(jax.random.fold_in(keys[17], 71), 0)
    edge_geom = jnp.clip(jax.random.uniform(keys[6], (GEO, EDGES), jnp.float32, -1.0, 1.0) * levels(keys[6], (GEO, EDGES), ((1, 32),), -0.4, 0.0), -1.0, 1.0).astype(jnp.bfloat16)
    mesh_init = bell_draw(keys[7], (MESH, D), 1.0, 6.0, ((0, 32),))
    neighbours = draw_neighbours(jax.random.fold_in(keys[17], 71), 0)
    grid_weight = bell_draw(keys[9], (VARS, D), VARS ** -0.5, 0.625)
    edge_weight = bell_draw(keys[10], (GEO, D), GEO ** -0.5, 3.0)
    message_weight = bell_draw(keys[11], (D, D), D ** -0.5, 0.25)
    enc_gain = jnp.clip(1.0 + 0.1 * jax.random.normal(keys[12], (D,), jnp.float32), 0.5, 1.5)
    att_gain = jnp.clip(1.0 + 0.1 * jax.random.normal(keys[13], (D,), jnp.float32), 0.5, 1.5)
    qkv_weight = bell_draw(keys[14], (D, 3 * D), D ** -0.5, 0.25)
    out_weight = bell_draw(keys[15], (D, D), D ** -0.5, 0.25)
    cotangent = bell_draw(keys[16], (LEVELS, MESH, D), (3.0 / (LEVELS * MESH) ** 0.5), 0.1875, ((0, 8), (1, 32)))
    return {"target_state": target_state, "noise_field": noise_field, "level_index": level_index, "send_rows": send_rows, "edge_src": edge_src, "edge_dst": edge_dst, "edge_geom": edge_geom, "mesh_init": mesh_init, "neighbours": neighbours, "grid_weight": grid_weight, "edge_weight": edge_weight, "message_weight": message_weight, "enc_gain": enc_gain, "att_gain": att_gain, "qkv_weight": qkv_weight, "out_weight": out_weight, "cotangent": cotangent}


sigma_max = 80.0
sigma_min = 0.03
plan_rho = 7.0
norm_eps = 1e-05
head_eps = 1e-06

def noise_level(index):
    upper_root = sigma_max ** (1.0 / plan_rho)
    lower_root = sigma_min ** (1.0 / plan_rho)
    fraction = index.astype(jnp.float32) / (PLAN - 1)
    return (upper_root + fraction * (lower_root - upper_root)) ** plan_rho

def rms_scale(values, gain, epsilon):
    return values * lax.rsqrt(lax.optimization_barrier(jnp.mean(values * values, axis=-1, keepdims=True)) + epsilon) * gain

def head_unit(values):
    shaped = values.reshape(values.shape[0], HEADS, HEAD_DIM)
    return (shaped * lax.rsqrt(lax.optimization_barrier(jnp.mean(shaped * shaped, axis=-1, keepdims=True)) + head_eps)).astype(jnp.bfloat16)

def reference(target_state, noise_field, level_index, send_rows, edge_src, edge_dst, edge_geom, mesh_init, neighbours, grid_weight, edge_weight, message_weight, enc_gain, att_gain, qkv_weight, out_weight, cotangent):
    contract = (((0,), (0,)), ((), ()))
    edge_ids = jnp.arange(EDGES, dtype=jnp.int32)
    owner_region = edge_ids // EDGES_DEV
    source_band = edge_src // SLOT
    slot_pos = edge_src % SLOT
    src_point = source_band * G_DEV + send_rows[source_band, owner_region, slot_pos]
    message_full = message_weight.astype(jnp.float32)

    def one_level(inputs):
        noise_one, index_one, cot_one = inputs
        sigma_level = noise_level(index_one)
        grid_in = ((target_state.astype(jnp.float32) + sigma_level * noise_one.astype(jnp.float32)) / jnp.sqrt(1.0 + sigma_level * sigma_level)).astype(jnp.bfloat16)

        def one_region(region_pos):
            first = region_pos * EDGES_DEV
            points = lax.dynamic_slice_in_dim(src_point, first, EDGES_DEV)
            columns = jnp.take(grid_in, points, axis=1)
            embedded = lax.dot_general(columns, grid_weight, contract, preferred_element_type=jnp.float32).astype(jnp.bfloat16)
            geometry = lax.dynamic_slice_in_dim(edge_geom, first, EDGES_DEV, 1)
            edge_terms = lax.dot_general(geometry, edge_weight, contract, preferred_element_type=jnp.float32)
            hidden = jax.nn.silu(embedded.astype(jnp.float32) + edge_terms).astype(jnp.bfloat16)
            dest_node = lax.dynamic_slice_in_dim(edge_dst, first, EDGES_DEV)
            hidden_sum = jax.ops.segment_sum(hidden.astype(jnp.float32), dest_node, num_segments=M_DEV + 1)[:M_DEV]
            return jnp.dot(hidden_sum, message_full, precision=lax.Precision.HIGHEST)
        aggregate = lax.map(one_region, jnp.arange(N_REGION, dtype=jnp.int32)).reshape(MESH, D)
        encoded = mesh_init.astype(jnp.float32) + rms_scale(aggregate, enc_gain, norm_eps)
        normed = rms_scale(encoded, att_gain, norm_eps).astype(jnp.bfloat16)
        projected = jnp.dot(normed, qkv_weight, preferred_element_type=jnp.float32)
        query_unit = head_unit(projected[:, :D])
        key_unit = head_unit(projected[:, D:2 * D])
        value_heads = projected[:, 2 * D:].astype(jnp.bfloat16).reshape(MESH, HEADS, HEAD_DIM)

        def one_block(region_pos):
            first = region_pos * M_DEV
            queries = lax.dynamic_slice_in_dim(query_unit, first, M_DEV).astype(jnp.float32)
            nearby = lax.dynamic_slice_in_dim(neighbours, first, M_DEV)
            keys_near = jnp.take(key_unit, nearby, axis=0).astype(jnp.float32)
            values_near = jnp.take(value_heads, nearby, axis=0).astype(jnp.float32)
            scores = jnp.einsum('bhd,bkhd->bhk', queries, keys_near) / math.sqrt(HEAD_DIM)
            weights = jnp.exp(scores)
            weights = (weights / lax.optimization_barrier(jnp.sum(weights, axis=-1, keepdims=True))).astype(jnp.bfloat16)
            mixed = jnp.einsum('bhk,bkhd->bhd', weights.astype(jnp.float32), values_near)
            return mixed.reshape(M_DEV, D).astype(jnp.bfloat16)
        attended = lax.map(one_block, jnp.arange(N_REGION, dtype=jnp.int32)).reshape(MESH, D)
        mesh_level = (encoded + jnp.dot(attended, out_weight, preferred_element_type=jnp.float32)).astype(jnp.bfloat16)
        partial_value = lax.dot_general(attended, cot_one, contract, preferred_element_type=jnp.float32)
        return (mesh_level, partial_value)
    mesh_out, partials = lax.map(one_level, (noise_field, level_index, cotangent))
    return (mesh_out, lax.optimization_barrier(jnp.sum(partials, axis=0)))
```

```python
import math

import jax
import jax.numpy as jnp
from jax import lax
from jax.experimental import pallas as pl
from jax.experimental.pallas import tpu as pltpu
from jax.sharding import PartitionSpec as P

BF = jnp.bfloat16
F32 = jnp.float32

D = 512
HEADS = 4
HEAD = 128
VARS = 84
VPAD = 96
GEO = 4
PLAN = 20
K_NB = 32
HALO = 128
NODES = 256
GRID = 2048
EDGES = 4096
SLOT = 128
REGIONS = 32
PLANES = 8
ROWS = 4
XS = 4
ETILE = 512
HALF = GRID // 2
KCAT = 128

sigma_max = 80.0
sigma_min = 0.03
plan_rho = 7.0
norm_eps = 1e-05
head_eps = 1e-06

UP_ROOT = sigma_max ** (1.0 / plan_rho)
LOW_ROOT = sigma_min ** (1.0 / plan_rho)

NT = (((1,), (1,)), ((), ()))


def dot(a, b):
    return jnp.dot(a, b, preferred_element_type=F32)


def dot_nt(a, b):
    return lax.dot_general(a, b, NT, preferred_element_type=F32)


def one_hot(code_row, rows):
    n = code_row.shape[1]
    ids = lax.broadcasted_iota(jnp.int32, (rows, n), 0).astype(F32).astype(BF)
    want = jnp.broadcast_to(code_row, (rows, n))
    return jnp.where(ids == want, jnp.ones((), BF), jnp.zeros((), BF))


def lanes(ref, first, count):
    return jnp.concatenate([ref[pl.ds(first + k, 1), :] for k in range(count)], axis=1)


def rms(values, epsilon):
    return values * lax.rsqrt(jnp.mean(values * values, axis=-1, keepdims=True) + epsilon)


def units(projected):
    return [
        rms(projected[:, h * HEAD : (h + 1) * HEAD], head_eps).astype(BF) for h in range(HEADS)
    ]


def with_ones(values):
    return jnp.concatenate([values, jnp.ones(values.shape, BF)], axis=1)


def plane_offset(i):
    half = lax.div(i + 1, 2)
    return lax.rem(4 + half * (1 - 2 * lax.rem(i, 2)) + PLANES, PLANES)


def kernel(
    level_ref,
    send_hbm,
    esrc_hbm,
    edst_hbm,
    nb_hbm,
    target_hbm,
    noise_hbm,
    geom_hbm,
    mesh_hbm,
    gw_hbm,
    ew_hbm,
    mw_hbm,
    eg_hbm,
    ag_hbm,
    qkv_hbm,
    ow_hbm,
    cot_hbm,
    mesh_out_ref,
    grad_ref,
    send_v,
    esrc_v,
    edst_v,
    nb_v,
    target_v,
    noise_v,
    geom_v,
    mesh_v,
    gw_v,
    ew_v,
    mw_v,
    eg_v,
    ag_v,
    qkv_v,
    ow_v,
    cot_v,
    in_sem,
    g_v,
    sbuf,
    rbuf,
    code_v,
    jbit_v,
    dstf_v,
    wc_v,
    wt_v,
    acc_v,
    node_v,
    hid_v,
    count_l,
    count_h,
    enc_v,
    nrm_v,
    halo_v,
    att_v,
    attt_v,
    a2a_send,
    a2a_recv,
    halo_send,
    halo_recv,
    p_v,
    sb1,
    rb1,
    sb2,
    rb2,
    own3,
    sb3,
    rb3,
    fbuf,
    s1_send,
    s1_recv,
    s2_send,
    s2_recv,
    s3_send,
    s3_recv,
    g3_send,
    g3_recv,
    g2_send,
    g2_recv,
    g1_send,
    g1_recv,
):
    noise = lax.axis_index("noise")
    me = lax.axis_index("region")
    core = lax.rem(noise, 2)
    mx = lax.div(noise, 2)
    mz = lax.div(me, ROWS)
    partner = noise + 1 - 2 * core
    region_next = lax.rem(me + 1, REGIONS)
    region_prev = lax.rem(me + REGIONS - 1, REGIONS)

    def x_peer(d):
        return lax.rem(mx + d, XS) * 2 + core

    pairs = [
        (noise_hbm.at[0], noise_v),
        (target_hbm, target_v),
        (send_hbm.at[0], send_v),
        (esrc_hbm, esrc_v),
        (edst_hbm, edst_v),
        (nb_hbm, nb_v),
        (geom_hbm, geom_v),
        (gw_hbm, gw_v),
        (ew_hbm, ew_v),
        (mw_hbm, mw_v),
        (mesh_hbm, mesh_v),
        (eg_hbm, eg_v),
        (ag_hbm, ag_v),
        (qkv_hbm, qkv_v),
        (cot_hbm.at[0], cot_v),
        (ow_hbm, ow_v),
    ]
    loads = [pltpu.make_async_copy(s, d, in_sem.at[i]) for i, (s, d) in enumerate(pairs)]
    (
        ld_noise,
        ld_target,
        ld_send,
        ld_esrc,
        ld_edst,
        ld_nb,
        ld_geom,
        ld_gw,
        ld_ew,
        ld_mw,
        ld_mesh,
        ld_eg,
        ld_ag,
        ld_qkv,
        ld_cot,
        ld_ow,
    ) = loads
    for load in loads:
        load.start()

    barrier = pltpu.get_barrier_semaphore()

    def tell(i, carry):
        pl.semaphore_signal(
            barrier,
            inc=1,
            device_id={"region": lax.rem(me + i, REGIONS)},
            device_id_type=pl.DeviceIdType.MESH,
        )
        return carry

    lax.fori_loop(1, REGIONS, tell, 0)
    for d in range(1, XS):
        pl.semaphore_signal(
            barrier, inc=1, device_id={"noise": x_peer(d)}, device_id_type=pl.DeviceIdType.MESH
        )
    pl.semaphore_signal(
        barrier, inc=1, device_id={"noise": partner}, device_id_type=pl.DeviceIdType.MESH
    )

    g_v[80:96, :] = jnp.zeros((16, HALF), BF)
    g_v[176:192, :] = jnp.zeros((16, HALF), BF)
    level = level_ref[0].astype(F32) * (1.0 / (PLAN - 1))
    root = UP_ROOT + level * (LOW_ROOT - UP_ROOT)
    root2 = root * root
    sigma = root2 * root2 * root2 * root
    ld_noise.wait()
    ld_target.wait()
    scale = lax.rsqrt(jnp.full((1, HALF), 1.0 + sigma * sigma, F32))
    for part in range(2):
        cols = slice(part * HALF, (part + 1) * HALF)
        noised = (
            target_v[:, cols].astype(F32) + sigma * noise_v[:, cols].astype(F32)
        ) * scale
        g_v[part * VPAD : part * VPAD + VARS, :] = noised.astype(BF)
    ld_send.wait()
    pl.semaphore_wait(barrier, REGIONS - 1 + XS - 1 + 1)

    def send_plane(i, carry):
        z = lax.rem(mz + plane_offset(i), PLANES)
        idx = lanes(send_v, ROWS * z, ROWS)
        upper = idx >= HALF
        low = jnp.where(upper, idx - HALF, idx).astype(F32)
        hot = jnp.concatenate(
            [one_hot((low - 256.0 * k).astype(BF), 256) for k in range(HALF // 256)], axis=0
        )
        both = dot(g_v[...], hot)
        picked = jnp.where(upper, both[VPAD:, :], both[:VPAD, :]).astype(BF)
        for k in range(ROWS):
            r = ROWS * z + k
            sbuf[r] = picked[:, k * SLOT : (k + 1) * SLOT]

            @pl.when(r != me)
            def _():
                pltpu.make_async_remote_copy(
                    src_ref=sbuf.at[r],
                    dst_ref=rbuf.at[me],
                    send_sem=a2a_send,
                    recv_sem=a2a_recv.at[mz],
                    device_id={"region": r},
                    device_id_type=pl.DeviceIdType.MESH,
                ).start()

            @pl.when(r == me)
            def _():
                pltpu.make_async_copy(sbuf.at[r], rbuf.at[me], a2a_recv.at[mz]).start()

        return carry

    with jax.named_scope("send_columns"):
        lax.fori_loop(0, PLANES, send_plane, 0)

    with jax.named_scope("tables"):
        ld_esrc.wait()
        ld_edst.wait()
        src = esrc_v[...]
        code_v[...] = (
            (src >> 9) * 256 + ((src >> 8) & 1) * 128 + (src & 127)
        ).astype(F32)
        jbit_v[...] = (src >> 7) & 1
        dstf_v[...] = edst_v[...].astype(F32)
        acc_v[...] = jnp.zeros((KCAT, EDGES), BF)
        ld_geom.wait()
        acc_v[VPAD : VPAD + GEO, :] = geom_v[...]
        ld_gw.wait()
        ld_ew.wait()
        wc_v[...] = jnp.zeros((KCAT, D), F32)
        wc_v[0:VARS, :] = gw_v[...].astype(F32)
        wc_v[VPAD : VPAD + GEO, :] = ew_v[...].astype(F32)
        wt_v[...] = wc_v[...].T.astype(BF)
        for e in range(EDGES // ETILE):
            row = lanes(dstf_v, e * (ETILE // 128), ETILE // 128).astype(BF)
            node_v[:, e * ETILE : (e + 1) * ETILE] = one_hot(row, NODES)
        ld_nb.wait()
        local = nb_v[...] - me * NODES + HALO
        local = jnp.where(local < 0, local + NODES * REGIONS, local)
        local = jnp.where(local >= NODES * REGIONS, local - NODES * REGIONS, local)
        for block in range(NODES // 32):
            rows = slice(block * 32, (block + 1) * 32)
            ids = lax.broadcasted_iota(jnp.int32, (32, NODES), 1)
            ids_l = ids + HALO
            ids_h = jnp.where(ids < HALO, ids, ids + NODES)
            total_l = jnp.zeros((32, NODES), F32)
            total_h = jnp.zeros((32, NODES), F32)
            for j in range(K_NB):
                at = local[rows, j : j + 1]
                total_l = total_l + jnp.where(ids_l == at, 1.0, 0.0)
                total_h = total_h + jnp.where(ids_h == at, 1.0, 0.0)
            count_l[rows, :] = total_l
            count_h[rows, :] = total_h

    def gather_plane(i, carry):
        z = lax.rem(mz + PLANES - plane_offset(i), PLANES)
        window = rbuf.at[pl.ds(ROWS * z, ROWS)]
        pltpu.make_async_copy(window, window, a2a_recv.at[z]).wait()
        table = jnp.concatenate(
            [
                jnp.concatenate([rbuf[ROWS * z], rbuf[ROWS * z + 1]], axis=0),
                jnp.concatenate([rbuf[ROWS * z + 2], rbuf[ROWS * z + 3]], axis=0),
            ],
            axis=1,
        )
        base = (z * 256).astype(F32)
        for e in range(EDGES // ETILE):
            first = e * (ETILE // 128)
            cols = slice(e * ETILE, (e + 1) * ETILE)
            hot = one_hot((lanes(code_v, first, ETILE // 128) - base).astype(BF), 256)
            both = dot(table, hot)
            odd = lanes(jbit_v, first, ETILE // 128) == 1
            picked = jnp.where(odd, both[VPAD:, :], both[:VPAD, :]).astype(BF)
            acc_v[0:VPAD, cols] = acc_v[0:VPAD, cols] + picked
        return carry

    with jax.named_scope("gather_edges"):
        lax.fori_loop(0, PLANES, gather_plane, 0)

    with jax.named_scope("hidden"):
        for e in range(EDGES // ETILE):
            cols = slice(e * ETILE, (e + 1) * ETILE)
            x = dot(wt_v[...], acc_v[:, cols])
            half = 0.5 * x
            hid_v[:, cols] = (half + half * jnp.tanh(half)).astype(BF)
        hidden_sum = dot_nt(node_v[...], hid_v[...])

    with jax.named_scope("encode"):
        ld_mw.wait()
        ld_mesh.wait()
        ld_eg.wait()
        ld_ag.wait()
        high = hidden_sum.astype(BF)
        rest = (hidden_sum - high.astype(F32)).astype(BF)
        aggregate = dot(high, mw_v[...]) + dot(rest, mw_v[...])
        encoded = mesh_v[...].astype(F32) + rms(aggregate, norm_eps) * eg_v[...]
        enc_v[...] = encoded
        nrm_v[...] = (rms(encoded, norm_eps) * ag_v[...]).astype(BF)

    to_prev = pltpu.make_async_remote_copy(
        src_ref=nrm_v.at[0:HALO],
        dst_ref=halo_v.at[HALO : 2 * HALO],
        send_sem=halo_send.at[0],
        recv_sem=halo_recv.at[0],
        device_id={"region": region_prev},
        device_id_type=pl.DeviceIdType.MESH,
    )
    to_next = pltpu.make_async_remote_copy(
        src_ref=nrm_v.at[NODES - HALO : NODES],
        dst_ref=halo_v.at[0:HALO],
        send_sem=halo_send.at[1],
        recv_sem=halo_recv.at[1],
        device_id={"region": region_next},
        device_id_type=pl.DeviceIdType.MESH,
    )
    to_prev.start()
    to_next.start()

    with jax.named_scope("attention_local"):
        ld_qkv.wait()
        projected = dot(nrm_v[...], qkv_v[...])
        query = units(projected[:, :D])
        key = units(projected[:, D : 2 * D])
        value = projected[:, 2 * D :].astype(BF)
        rate = 1.0 / math.sqrt(HEAD)

        def mix(q, k, v, count):
            weight = (jnp.exp(dot_nt(q, k) * rate) * count).astype(BF)
            return dot(weight, with_ones(v))

        mixed = [
            mix(query[h], key[h], value[:, h * HEAD : (h + 1) * HEAD], count_l[...])
            for h in range(HEADS)
        ]

    with jax.named_scope("attention_halo"):
        to_prev.wait()
        to_next.wait()
        beside = dot(halo_v[...], qkv_v[:, D:])
        key = units(beside[:, :D])
        value = beside[:, D:].astype(BF)
        for h in range(HEADS):
            both = mixed[h] + mix(
                query[h], key[h], value[:, h * HEAD : (h + 1) * HEAD], count_h[...]
            )
            att_v[:, h * HEAD : (h + 1) * HEAD] = both[:, :HEAD] / both[:, HEAD:]
        attt_v[...] = att_v[...].T.astype(BF)

    def quarter(i):
        return lax.rem(mx + (2, 1, 3, 0)[i], XS)

    with jax.named_scope("gradient_term"):
        ld_cot.wait()
        other = pl.multiple_of((1 - core) * NODES, NODES)
        mine = pl.multiple_of(core * NODES, NODES)
        sb1[...] = dot(attt_v[pl.ds(other, NODES), :], cot_v[...]).astype(BF)
        firsts = []
        for i in range(XS):
            rows = pl.ds(pl.multiple_of(quarter(i) * 64, 64), 64)
            copy = pltpu.make_async_remote_copy(
                src_ref=sb1.at[rows],
                dst_ref=rb1.at[rows],
                send_sem=s1_send.at[i],
                recv_sem=s1_recv.at[i],
                device_id={"noise": partner},
                device_id_type=pl.DeviceIdType.MESH,
            )
            copy.start()
            firsts.append(copy)
        p_v[...] = dot(attt_v[pl.ds(mine, NODES), :], cot_v[...])

    with jax.named_scope("reduce_x"):
        seconds = []
        for i in range(XS):
            rows = pl.ds(pl.multiple_of(quarter(i) * 64, 64), 64)
            firsts[i].wait_recv()
            total = p_v[rows, :] + rb1[rows, :].astype(F32)
            if i < XS - 1:
                d = (2, 1, 3)[i]
                sb2[i] = total.astype(BF)
                copy = pltpu.make_async_remote_copy(
                    src_ref=sb2.at[i],
                    dst_ref=rb2.at[i],
                    send_sem=s2_send.at[i],
                    recv_sem=s2_recv.at[i],
                    device_id={"noise": x_peer(d)},
                    device_id_type=pl.DeviceIdType.MESH,
                )
                copy.start()
                seconds.append(copy)
            else:
                own3[...] = total

    with jax.named_scope("mesh_out"):
        ld_ow.wait()
        mesh_out_ref[...] = (
            enc_v[...] + dot(att_v[...].astype(BF), ow_v[...])
        ).astype(BF)

    tile_me = lax.div(me, 2)
    owner = lax.rem(me, 2) == core

    def tile_of(t):
        return (
            pl.ds(pl.multiple_of(lax.div(t, 4) * 16, 16), 16),
            pl.ds(pl.multiple_of(lax.rem(t, 4) * 128, 128), 128),
        )

    with jax.named_scope("reduce_region"):
        for copy in seconds:
            copy.wait_recv()
        total = own3[...]
        for i in range(XS - 1):
            total = total + rb2[i].astype(F32)
        own3[...] = total
        sb3[...] = total.astype(BF)

        def send_tile(i, carry):
            t = lax.rem(tile_me + i, 16)
            to = 2 * t + core
            rows, cols = tile_of(t)

            @pl.when(to != me)
            def _():
                pltpu.make_async_remote_copy(
                    src_ref=sb3.at[rows, cols],
                    dst_ref=rb3.at[lax.rem(me - to + REGIONS, REGIONS) - 1],
                    send_sem=s3_send,
                    recv_sem=s3_recv,
                    device_id={"region": to},
                    device_id_type=pl.DeviceIdType.MESH,
                ).start()

            return carry

        lax.fori_loop(0, 16, send_tile, 0)

    quarter_row = pl.multiple_of(core * NODES + mx * 64, 64)
    own_rows = pl.ds(pl.multiple_of(quarter_row + lax.div(tile_me, 4) * 16, 16), 16)
    own_cols = pl.ds(pl.multiple_of(lax.rem(tile_me, 4) * 128, 128), 128)

    with jax.named_scope("gather_region"):

        @pl.when(owner)
        def _():
            pltpu.make_async_copy(rb3, rb3, s3_recv).wait()
            rows, cols = tile_of(tile_me)
            total = own3[rows, cols]
            for i in range(REGIONS - 1):
                total = total + rb3[i].astype(F32)
            fbuf[own_rows, own_cols] = total.astype(BF)

            def send_own(i, carry):
                pltpu.make_async_remote_copy(
                    src_ref=fbuf.at[own_rows, own_cols],
                    dst_ref=fbuf.at[own_rows, own_cols],
                    send_sem=g3_send,
                    recv_sem=g3_recv,
                    device_id={"region": lax.rem(me + i, REGIONS)},
                    device_id_type=pl.DeviceIdType.MESH,
                ).start()
                return carry

            lax.fori_loop(1, REGIONS, send_own, 0)
            got = rb3.at[0:15]
            pltpu.make_async_copy(got, got, g3_recv).wait()

        @pl.when(jnp.logical_not(owner))
        def _():
            got = rb3.at[0:16]
            pltpu.make_async_copy(got, got, g3_recv).wait()

    with jax.named_scope("gather_x"):
        mine4 = pl.ds(quarter_row, 64)
        thirds = []
        for i, d in enumerate((2, 1, 3)):
            copy = pltpu.make_async_remote_copy(
                src_ref=fbuf.at[mine4],
                dst_ref=fbuf.at[mine4],
                send_sem=g2_send.at[i],
                recv_sem=g2_recv.at[i],
                device_id={"noise": x_peer(d)},
                device_id_type=pl.DeviceIdType.MESH,
            )
            copy.start()
            thirds.append(copy)
        lasts = []
        for i, d in enumerate((0, 1, 3, 2)):
            rows = pl.ds(pl.multiple_of(core * NODES + lax.rem(mx + XS - d, XS) * 64, 64), 64)
            if d:
                thirds[(2, 1, 3).index(d)].wait_recv()
            copy = pltpu.make_async_remote_copy(
                src_ref=fbuf.at[rows],
                dst_ref=fbuf.at[rows],
                send_sem=g1_send.at[i],
                recv_sem=g1_recv.at[i],
                device_id={"noise": partner},
                device_id_type=pl.DeviceIdType.MESH,
            )
            copy.start()
            lasts.append(copy)
        for copy in lasts:
            copy.wait_recv()
        grad_ref[...] = fbuf[...]

    sent = sbuf.at[0 : REGIONS - 1]
    pltpu.make_async_copy(sent, sent, a2a_send).wait()
    for copy in firsts + seconds + thirds + lasts:
        copy.wait_send()

    @pl.when(owner)
    def _():
        pltpu.make_async_copy(rb3, rb3, g3_send).wait()
        some = rb3.at[0:15]
        pltpu.make_async_copy(some, some, s3_send).wait()

    @pl.when(jnp.logical_not(owner))
    def _():
        some = rb3.at[0:16]
        pltpu.make_async_copy(some, some, s3_send).wait()


def body(
    target_state,
    noise_field,
    level_index,
    send_rows,
    edge_src,
    edge_dst,
    edge_geom,
    mesh_init,
    neighbours,
    grid_weight,
    edge_weight,
    message_weight,
    enc_gain,
    att_gain,
    qkv_weight,
    out_weight,
    cotangent,
):
    operands = (
        level_index,
        send_rows,
        edge_src.reshape(EDGES // 128, 128),
        edge_dst.reshape(EDGES // 128, 128),
        neighbours,
        target_state,
        noise_field,
        edge_geom,
        mesh_init,
        grid_weight,
        edge_weight,
        message_weight,
        enc_gain.reshape(1, D),
        att_gain.reshape(1, D),
        qkv_weight,
        out_weight,
        cotangent,
    )
    vmem = pltpu.VMEM
    dma = pltpu.SemaphoreType.DMA
    i32 = jnp.int32
    scratch = [
        vmem((REGIONS, SLOT), i32),
        vmem((EDGES // 128, 128), i32),
        vmem((EDGES // 128, 128), i32),
        vmem((NODES, K_NB), i32),
        vmem((VARS, GRID), BF),
        vmem((VARS, GRID), BF),
        vmem((GEO, EDGES), BF),
        vmem((NODES, D), BF),
        vmem((VARS, D), BF),
        vmem((GEO, D), BF),
        vmem((D, D), BF),
        vmem((1, D), F32),
        vmem((1, D), F32),
        vmem((D, 3 * D), BF),
        vmem((D, D), BF),
        vmem((NODES, D), BF),
        dma((16,)),
        vmem((2 * VPAD, HALF), BF),
        vmem((REGIONS, VPAD, SLOT), BF),
        vmem((REGIONS, VPAD, SLOT), BF),
        vmem((EDGES // 128, 128), F32),
        vmem((EDGES // 128, 128), i32),
        vmem((EDGES // 128, 128), F32),
        vmem((KCAT, D), F32),
        vmem((D, KCAT), BF),
        vmem((KCAT, EDGES), BF),
        vmem((NODES, EDGES), BF),
        vmem((D, EDGES), BF),
        vmem((NODES, NODES), F32),
        vmem((NODES, NODES), F32),
        vmem((NODES, D), F32),
        vmem((NODES, D), BF),
        vmem((2 * HALO, D), BF),
        vmem((NODES, D), F32),
        vmem((D, NODES), BF),
        dma,
        dma((PLANES,)),
        dma((2,)),
        dma((2,)),
        vmem((NODES, D), F32),
        vmem((NODES, D), BF),
        vmem((NODES, D), BF),
        vmem((XS - 1, 64, D), BF),
        vmem((XS - 1, 64, D), BF),
        vmem((64, D), F32),
        vmem((64, D), BF),
        vmem((REGIONS - 1, 16, 128), BF),
        vmem((D, D), BF),
        dma((XS,)),
        dma((XS,)),
        dma((XS - 1,)),
        dma((XS - 1,)),
        dma,
        dma,
        dma,
        dma,
        dma((XS - 1,)),
        dma((XS - 1,)),
        dma((XS,)),
        dma((XS,)),
    ]
    mesh_out, grad = pl.pallas_call(
        kernel,
        out_shape=(
            jax.ShapeDtypeStruct((NODES, D), BF),
            jax.ShapeDtypeStruct((D, D), BF),
        ),
        in_specs=[pl.BlockSpec(memory_space=pltpu.SMEM)]
        + [pl.BlockSpec(memory_space=pl.ANY)] * (len(operands) - 1),
        out_specs=(
            pl.BlockSpec(memory_space=pltpu.VMEM),
            pl.BlockSpec(memory_space=pltpu.VMEM),
        ),
        scratch_shapes=scratch,
        compiler_params=pltpu.CompilerParams(
            collective_id=0, has_side_effects=True, vmem_limit_bytes=60 * 1024 * 1024
        ),
        cost_estimate=pl.CostEstimate(
            flops=12_000_000_000, bytes_accessed=6_000_000, transcendentals=3_000_000
        ),
    )(*operands)
    return mesh_out[None], grad.astype(F32)


def solution(mesh):
    in_specs = (
        P(None, "region"),
        P("noise", None, "region"),
        P("noise"),
        P("region", None, None),
        P("region"),
        P("region"),
        P(None, "region"),
        P("region", None),
        P("region", None),
        P(),
        P(),
        P(),
        P(),
        P(),
        P(),
        P(),
        P("noise", "region", None),
    )
    out_specs = (P("noise", "region", None), P())
    return jax.shard_map(body, mesh=mesh, in_specs=in_specs, out_specs=out_specs, check_vma=False)
```

```python
import math

import jax
import jax.numpy as jnp
from jax import lax
from jax.experimental import pallas as pl
from jax.experimental.pallas import tpu as pltpu
from jax.sharding import PartitionSpec as P

BF = jnp.bfloat16
F32 = jnp.float32

D = 512
HEADS = 4
HEAD = 128
VARS = 84
VPAD = 96
GEO = 4
PLAN = 20
K_NB = 32
HALO = 128
NODES = 256
GRID = 2048
EDGES = 4096
SLOT = 128
REGIONS = 32
PLANES = 8
ROWS = 4
XS = 4
ETILE = 512
HSPLIT = 8
HALF = GRID // 2
KCAT = 128

sigma_max = 80.0
sigma_min = 0.03
plan_rho = 7.0
norm_eps = 1e-05
head_eps = 1e-06

UP_ROOT = sigma_max ** (1.0 / plan_rho)
LOW_ROOT = sigma_min ** (1.0 / plan_rho)

AROUND = sorted(
    [(dx, dy) for dx in range(XS) for dy in range(ROWS) if dx or dy],
    key=lambda d: (-min(d[0], XS - d[0]) - min(d[1], ROWS - d[1]), d),
)

NT = (((1,), (1,)), ((), ()))


def dot(a, b):
    return jnp.dot(a, b, preferred_element_type=F32)


def dot_nt(a, b):
    return lax.dot_general(a, b, NT, preferred_element_type=F32)


def one_hot(code_row, rows):
    n = code_row.shape[1]
    ids = lax.broadcasted_iota(jnp.int32, (rows, n), 0).astype(F32).astype(BF)
    want = jnp.broadcast_to(code_row, (rows, n))
    return jnp.where(ids == want, jnp.ones((), BF), jnp.zeros((), BF))


def lanes(ref, first, count):
    return jnp.concatenate([ref[pl.ds(first + k, 1), :] for k in range(count)], axis=1)


def rms(values, epsilon):
    return values * lax.rsqrt(jnp.mean(values * values, axis=-1, keepdims=True) + epsilon)


def units(projected):
    return [
        rms(projected[:, h * HEAD : (h + 1) * HEAD], head_eps).astype(BF) for h in range(HEADS)
    ]


def with_ones(values):
    return jnp.concatenate([values, jnp.ones(values.shape, BF)], axis=1)


def plane_offset(i):
    half = lax.div(i + 1, 2)
    return lax.rem(4 + half * (1 - 2 * lax.rem(i, 2)) + PLANES, PLANES)


def kernel(
    level_ref,
    send_hbm,
    esrc_hbm,
    edst_hbm,
    nb_hbm,
    target_hbm,
    noise_hbm,
    geom_hbm,
    mesh_hbm,
    gw_hbm,
    ew_hbm,
    mw_hbm,
    eg_hbm,
    ag_hbm,
    qkv_hbm,
    ow_hbm,
    cot_hbm,
    mesh_out_ref,
    grad_ref,
    send_v,
    esrc_v,
    edst_v,
    nb_v,
    target_v,
    noise_v,
    geom_v,
    mesh_v,
    gw_v,
    ew_v,
    mw_v,
    eg_v,
    ag_v,
    qkv_v,
    ow_v,
    cot_v,
    in_sem,
    g_v,
    sbuf,
    rbuf,
    code_v,
    jbit_v,
    dstf_v,
    wc_v,
    wt_v,
    tab_v,
    acc_v,
    node_v,
    hid_v,
    count_t,
    count_l,
    count_h,
    enc_v,
    nrm_v,
    halo_v,
    att_v,
    attt_v,
    a2a_send,
    a2a_recv,
    halo_send,
    halo_recv,
    p_v,
    sb1,
    rb1,
    sb2,
    rb2,
    zbuf,
    fbuf,
    s1_send,
    s1_recv,
    s2_send,
    s2_recv,
    s3_send,
    s3_recv,
    g2_send,
    g2_recv,
    g1_send,
    g1_recv,
):
    noise = lax.axis_index("noise")
    me = lax.axis_index("region")
    core = lax.rem(noise, 2)
    mx = lax.div(noise, 2)
    mz = lax.div(me, ROWS)
    my = lax.rem(me, ROWS)
    partner = noise + 1 - 2 * core
    region_next = lax.rem(me + 1, REGIONS)
    region_prev = lax.rem(me + REGIONS - 1, REGIONS)

    def across(dx, dy):
        return {
            "noise": lax.rem(mx + dx, XS) * 2 + core,
            "region": mz * ROWS + lax.rem(my + dy, ROWS),
        }

    def piece(x, y):
        return pl.ds(pl.multiple_of((x * ROWS + y) * 16, 16), 16)

    pairs = [
        (noise_hbm.at[0], noise_v),
        (target_hbm, target_v),
        (send_hbm.at[0], send_v),
        (esrc_hbm, esrc_v),
        (edst_hbm, edst_v),
        (nb_hbm, nb_v),
        (geom_hbm, geom_v),
        (gw_hbm, gw_v),
        (ew_hbm, ew_v),
        (mw_hbm, mw_v),
        (mesh_hbm, mesh_v),
        (eg_hbm, eg_v),
        (ag_hbm, ag_v),
        (qkv_hbm, qkv_v),
        (cot_hbm.at[0], cot_v),
        (ow_hbm, ow_v),
    ]
    loads = [pltpu.make_async_copy(s, d, in_sem.at[i]) for i, (s, d) in enumerate(pairs)]
    (
        ld_noise,
        ld_target,
        ld_send,
        ld_esrc,
        ld_edst,
        ld_nb,
        ld_geom,
        ld_gw,
        ld_ew,
        ld_mw,
        ld_mesh,
        ld_eg,
        ld_ag,
        ld_qkv,
        ld_cot,
        ld_ow,
    ) = loads
    for load in loads[:3]:
        load.start()

    barrier = pltpu.get_barrier_semaphore()

    def tell(device):
        pl.semaphore_signal(
            barrier, inc=1, device_id=device, device_id_type=pl.DeviceIdType.MESH
        )

    def tell_region(i, carry):
        tell({"region": lax.rem(me + i, REGIONS)})
        return carry

    lax.fori_loop(1, REGIONS, tell_region, 0)
    beyond = [(dx, dy) for dx, dy in AROUND if dx]
    for dx, dy in beyond:
        tell(across(dx, dy))
    tell({"noise": partner})
    for load in loads[3:]:
        load.start()

    g_v[80:96, :] = jnp.zeros((16, HALF), BF)
    g_v[176:192, :] = jnp.zeros((16, HALF), BF)
    level = jnp.broadcast_to(level_ref[...], (1, HALF)).astype(F32) * (1.0 / (PLAN - 1))
    root = UP_ROOT + level * (LOW_ROOT - UP_ROOT)
    root2 = root * root
    sigma = root2 * root2 * root2 * root
    scale = lax.rsqrt(1.0 + sigma * sigma)
    ld_noise.wait()
    ld_target.wait()
    for part in range(2):
        cols = slice(part * HALF, (part + 1) * HALF)
        noised = (
            target_v[:, cols].astype(F32) + sigma * noise_v[:, cols].astype(F32)
        ) * scale
        g_v[part * VPAD : part * VPAD + VARS, :] = noised.astype(BF)
    ld_send.wait()
    pl.semaphore_wait(barrier, REGIONS - 1 + len(beyond) + 1)

    def send_plane(i, carry):
        z = lax.rem(mz + plane_offset(i), PLANES)
        idx = lanes(send_v, ROWS * z, ROWS)
        upper = idx >= HALF
        low = jnp.where(upper, idx - HALF, idx).astype(F32)
        hot = jnp.concatenate(
            [one_hot((low - 256.0 * k).astype(BF), 256) for k in range(HALF // 256)], axis=0
        )
        both = dot(g_v[...], hot)
        picked = jnp.where(upper, both[VPAD:, :], both[:VPAD, :]).astype(BF)
        for k in range(ROWS):
            r = ROWS * z + k
            sbuf[r] = picked[:VARS, k * SLOT : (k + 1) * SLOT]

            @pl.when(r != me)
            def _():
                pltpu.make_async_remote_copy(
                    src_ref=sbuf.at[r],
                    dst_ref=rbuf.at[me],
                    send_sem=a2a_send,
                    recv_sem=a2a_recv.at[mz],
                    device_id={"region": r},
                    device_id_type=pl.DeviceIdType.MESH,
                ).start()

            @pl.when(r == me)
            def _():
                pltpu.make_async_copy(sbuf.at[r], rbuf.at[me], a2a_recv.at[mz]).start()

        return carry

    with jax.named_scope("send_columns"):
        lax.fori_loop(0, PLANES, send_plane, 0)

    with jax.named_scope("tables"):
        ld_esrc.wait()
        ld_edst.wait()
        src = esrc_v[...]
        code_v[...] = (
            (src >> 9) * 256 + ((src >> 8) & 1) * 128 + (src & 127)
        ).astype(F32)
        jbit_v[...] = (src >> 7) & 1
        dstf_v[...] = edst_v[...].astype(F32)
        acc_v[...] = jnp.zeros((KCAT, EDGES), BF)
        tab_v[...] = jnp.zeros((2 * VPAD, 2 * SLOT), BF)
        ld_geom.wait()
        acc_v[VPAD : VPAD + GEO, :] = geom_v[...]
        ld_gw.wait()
        ld_ew.wait()
        wc_v[...] = jnp.zeros((KCAT, D), F32)
        wc_v[0:VARS, :] = gw_v[...].astype(F32)
        wc_v[VPAD : VPAD + GEO, :] = ew_v[...].astype(F32)
        wt_v[...] = wc_v[...].T.astype(BF)
        for e in range(EDGES // ETILE):
            row = lanes(dstf_v, e * (ETILE // 128), ETILE // 128).astype(BF)
            node_v[:, e * ETILE : (e + 1) * ETILE] = one_hot(row, NODES)
        ld_nb.wait()
        local = nb_v[...] - me * NODES + HALO
        local = jnp.where(local < 0, local + NODES * REGIONS, local)
        local = jnp.where(local >= NODES * REGIONS, local - NODES * REGIONS, local)
        for block in range(2 * NODES // 64):
            ids = lax.broadcasted_iota(jnp.int32, (64, NODES), 0) + block * 64
            total = jnp.zeros((64, NODES), F32)
            for j in range(K_NB):
                total = total + jnp.where(ids == local[j : j + 1, :], 1.0, 0.0)
            spot = slice(block * 64, (block + 1) * 64)
            count_t[spot, :] = total
        count_l[...] = count_t[HALO : HALO + NODES, :].T
        count_h[:, :HALO] = count_t[:HALO, :].T
        count_h[:, HALO:] = count_t[HALO + NODES :, :].T

    def gather_plane(i, carry):
        z = lax.rem(mz + PLANES - plane_offset(i), PLANES)
        window = rbuf.at[pl.ds(ROWS * z, ROWS)]
        pltpu.make_async_copy(window, window, a2a_recv.at[z]).wait()
        for k in range(ROWS):
            top, left = (k % 2) * VPAD, (k // 2) * SLOT
            tab_v[top : top + VARS, left : left + SLOT] = rbuf[ROWS * z + k]
        table = tab_v[...]
        base = (z * 256).astype(F32)
        for e in range(EDGES // ETILE):
            first = e * (ETILE // 128)
            cols = slice(e * ETILE, (e + 1) * ETILE)
            hot = one_hot((lanes(code_v, first, ETILE // 128) - base).astype(BF), 256)
            both = dot(table, hot)
            odd = lanes(jbit_v, first, ETILE // 128) == 1
            picked = jnp.where(odd, both[VPAD:, :], both[:VPAD, :]).astype(BF)
            acc_v[0:VPAD, cols] = acc_v[0:VPAD, cols] + picked
        return carry

    with jax.named_scope("gather_edges"):
        lax.fori_loop(0, PLANES, gather_plane, 0)

    with jax.named_scope("hidden"):
        for e in range(EDGES // ETILE):
            cols = slice(e * ETILE, (e + 1) * ETILE)
            x = dot(wt_v[...], acc_v[:, cols])
            half = 0.5 * x
            hid_v[:, cols] = (half + half * jnp.tanh(half)).astype(BF)
        hidden_sum = dot_nt(node_v[...], hid_v[...])

    with jax.named_scope("encode"):
        ld_mw.wait()
        ld_mesh.wait()
        ld_eg.wait()
        ld_ag.wait()
        high = hidden_sum.astype(BF)
        rest = (hidden_sum - high.astype(F32)).astype(BF)
        aggregate = dot(high, mw_v[...]) + dot(rest, mw_v[...])
        encoded = mesh_v[...].astype(F32) + rms(aggregate, norm_eps) * eg_v[...]
        enc_v[...] = encoded
        nrm_v[...] = (rms(encoded, norm_eps) * ag_v[...]).astype(BF)

    step = HALO // HSPLIT
    for part in range(HSPLIT):
        for side, first, there, to in (
            (0, 0, HALO, region_prev),
            (1, NODES - HALO, 0, region_next),
        ):
            pltpu.make_async_remote_copy(
                src_ref=nrm_v.at[first + part * step : first + (part + 1) * step],
                dst_ref=halo_v.at[there + part * step : there + (part + 1) * step],
                send_sem=halo_send,
                recv_sem=halo_recv,
                device_id={"region": to},
                device_id_type=pl.DeviceIdType.MESH,
            ).start()
    halo_sent = pltpu.make_async_copy(nrm_v, nrm_v, halo_send)
    halo_got = pltpu.make_async_copy(halo_v, halo_v, halo_recv)

    with jax.named_scope("attention_local"):
        ld_qkv.wait()
        projected = dot(nrm_v[...], qkv_v[...])
        query = units(projected[:, :D])
        key = units(projected[:, D : 2 * D])
        value = projected[:, 2 * D :].astype(BF)
        rate = 1.0 / math.sqrt(HEAD)

        def mix(q, k, v, count):
            weight = (jnp.exp(dot_nt(q, k) * rate) * count).astype(BF)
            return dot(weight, with_ones(v))

        mixed = [
            mix(query[h], key[h], value[:, h * HEAD : (h + 1) * HEAD], count_l[...])
            for h in range(HEADS)
        ]

    with jax.named_scope("attention_halo"):
        halo_got.wait()
        beside = dot(halo_v[...], qkv_v[:, D:])
        key = units(beside[:, :D])
        value = beside[:, D:].astype(BF)
        for h in range(HEADS):
            both = mixed[h] + mix(
                query[h], key[h], value[:, h * HEAD : (h + 1) * HEAD], count_h[...]
            )
            att_v[:, h * HEAD : (h + 1) * HEAD] = both[:, :HEAD] / both[:, HEAD:]
        attt_v[...] = att_v[...].T.astype(BF)

    with jax.named_scope("gradient_term"):
        ld_cot.wait()
        other = pl.multiple_of((1 - core) * NODES, NODES)
        mine = pl.multiple_of(core * NODES, NODES)
        sb1[...] = dot(attt_v[pl.ds(other, NODES), :], cot_v[...]).astype(BF)
        swap = pltpu.make_async_remote_copy(
            src_ref=sb1,
            dst_ref=rb1,
            send_sem=s1_send,
            recv_sem=s1_recv,
            device_id={"noise": partner},
            device_id_type=pl.DeviceIdType.MESH,
        )
        swap.start()
        p_v[...] = dot(attt_v[pl.ds(mine, NODES), :], cot_v[...])
        swap.wait_recv()

    with jax.named_scope("reduce_xy"):
        p_v[...] = p_v[...] + rb1[...].astype(F32)
        sb2[...] = p_v[...].astype(BF)
        for i, (dx, dy) in enumerate(AROUND):
            there = piece(lax.rem(mx + dx, XS), lax.rem(my + dy, ROWS))
            pltpu.make_async_remote_copy(
                src_ref=sb2.at[there],
                dst_ref=rb2.at[i],
                send_sem=s2_send,
                recv_sem=s2_recv,
                device_id=across(dx, dy),
                device_id_type=pl.DeviceIdType.MESH,
            ).start()

    with jax.named_scope("mesh_out"):
        ld_ow.wait()
        mesh_out_ref[...] = (
            enc_v[...] + dot(att_v[...].astype(BF), ow_v[...])
        ).astype(BF)

    with jax.named_scope("reduce_z"):
        pltpu.make_async_copy(rb2, rb2, s2_recv).wait()
        total = p_v[piece(mx, my), :]
        for i in range(len(AROUND)):
            total = total + rb2[i].astype(F32)
        zbuf[mz] = total.astype(BF)
        for d in (4, 3, 5, 2, 6, 1, 7):
            pltpu.make_async_remote_copy(
                src_ref=zbuf.at[mz],
                dst_ref=zbuf.at[mz],
                send_sem=s3_send,
                recv_sem=s3_recv,
                device_id={"region": lax.rem(me + ROWS * d, REGIONS)},
                device_id_type=pl.DeviceIdType.MESH,
            ).start()
        seven = zbuf.at[0 : PLANES - 1]
        pltpu.make_async_copy(seven, seven, s3_recv).wait()
        total = zbuf[0].astype(F32)
        for z in range(1, PLANES):
            total = total + zbuf[z].astype(F32)

    with jax.named_scope("gather_xy"):
        place = pl.ds(
            pl.multiple_of(core * NODES + (mx * ROWS + my) * 16, 16), 16
        )
        fbuf[place, :] = total.astype(BF)
        for dx, dy in AROUND:
            pltpu.make_async_remote_copy(
                src_ref=fbuf.at[place],
                dst_ref=fbuf.at[place],
                send_sem=g2_send,
                recv_sem=g2_recv,
                device_id=across(dx, dy),
                device_id_type=pl.DeviceIdType.MESH,
            ).start()
        pltpu.make_async_copy(rb2, rb2, g2_recv).wait()

    with jax.named_scope("gather_core"):
        half = pl.ds(mine, NODES)
        back = pltpu.make_async_remote_copy(
            src_ref=fbuf.at[half],
            dst_ref=fbuf.at[half],
            send_sem=g1_send,
            recv_sem=g1_recv,
            device_id={"noise": partner},
            device_id_type=pl.DeviceIdType.MESH,
        )
        back.start()
        back.wait_recv()
        grad_ref[...] = fbuf[...]

    sent = sbuf.at[0 : REGIONS - 1]
    pltpu.make_async_copy(sent, sent, a2a_send).wait()
    halo_sent.wait()
    swap.wait_send()
    pltpu.make_async_copy(rb2, rb2, s2_send).wait()
    pltpu.make_async_copy(seven, seven, s3_send).wait()
    pltpu.make_async_copy(rb2, rb2, g2_send).wait()
    back.wait_send()


def widen(mesh_hbm, grad_hbm, mesh_out_hbm, grad_out_hbm, narrow, wide, mesh_v, in_sems, out_sems):
    parts = [pl.ds(i * 128, 128) for i in range(4)]
    got = [
        pltpu.make_async_copy(grad_hbm.at[p], narrow.at[p], in_sems.at[i])
        for i, p in enumerate(parts)
    ]
    mesh_got = pltpu.make_async_copy(mesh_hbm, mesh_v, in_sems.at[4])
    for copy in got:
        copy.start()
    mesh_got.start()
    sent = []
    for i, p in enumerate(parts):
        got[i].wait()
        wide[p, :] = narrow[p, :].astype(F32)
        copy = pltpu.make_async_copy(wide.at[p], grad_out_hbm.at[p], out_sems.at[i])
        copy.start()
        sent.append(copy)
    mesh_got.wait()
    copy = pltpu.make_async_copy(mesh_v, mesh_out_hbm.at[0], out_sems.at[4])
    copy.start()
    for copy in sent + [copy]:
        copy.wait()


def body(
    target_state,
    noise_field,
    level_index,
    send_rows,
    edge_src,
    edge_dst,
    edge_geom,
    mesh_init,
    neighbours,
    grid_weight,
    edge_weight,
    message_weight,
    enc_gain,
    att_gain,
    qkv_weight,
    out_weight,
    cotangent,
):
    operands = (
        level_index.reshape(1, 1),
        send_rows,
        edge_src.reshape(EDGES // 128, 128),
        edge_dst.reshape(EDGES // 128, 128),
        neighbours.T,
        target_state,
        noise_field,
        edge_geom,
        mesh_init,
        grid_weight,
        edge_weight,
        message_weight,
        enc_gain.reshape(1, D),
        att_gain.reshape(1, D),
        qkv_weight,
        out_weight,
        cotangent,
    )
    vmem = pltpu.VMEM
    dma = pltpu.SemaphoreType.DMA
    i32 = jnp.int32
    scratch = [
        vmem((REGIONS, SLOT), i32),
        vmem((EDGES // 128, 128), i32),
        vmem((EDGES // 128, 128), i32),
        vmem((K_NB, NODES), i32),
        vmem((VARS, GRID), BF),
        vmem((VARS, GRID), BF),
        vmem((GEO, EDGES), BF),
        vmem((NODES, D), BF),
        vmem((VARS, D), BF),
        vmem((GEO, D), BF),
        vmem((D, D), BF),
        vmem((1, D), F32),
        vmem((1, D), F32),
        vmem((D, 3 * D), BF),
        vmem((D, D), BF),
        vmem((NODES, D), BF),
        dma((16,)),
        vmem((2 * VPAD, HALF), BF),
        vmem((REGIONS, VARS, SLOT), BF),
        vmem((REGIONS, VARS, SLOT), BF),
        vmem((EDGES // 128, 128), F32),
        vmem((EDGES // 128, 128), i32),
        vmem((EDGES // 128, 128), F32),
        vmem((KCAT, D), F32),
        vmem((D, KCAT), BF),
        vmem((2 * VPAD, 2 * SLOT), BF),
        vmem((KCAT, EDGES), BF),
        vmem((NODES, EDGES), BF),
        vmem((D, EDGES), BF),
        vmem((2 * NODES, NODES), F32),
        vmem((NODES, NODES), F32),
        vmem((NODES, NODES), F32),
        vmem((NODES, D), F32),
        vmem((NODES, D), BF),
        vmem((2 * HALO, D), BF),
        vmem((NODES, D), F32),
        vmem((D, NODES), BF),
        dma,
        dma((PLANES,)),
        dma,
        dma,
        vmem((NODES, D), F32),
        vmem((NODES, D), BF),
        vmem((NODES, D), BF),
        vmem((NODES, D), BF),
        vmem((len(AROUND), 16, D), BF),
        vmem((PLANES, 16, D), BF),
        vmem((D, D), BF),
    ] + [dma] * 10
    mesh_out, grad = pl.pallas_call(
        kernel,
        out_shape=(
            jax.ShapeDtypeStruct((NODES, D), BF),
            jax.ShapeDtypeStruct((D, D), BF),
        ),
        in_specs=[pl.BlockSpec(memory_space=pltpu.VMEM)]
        + [pl.BlockSpec(memory_space=pl.ANY)] * (len(operands) - 1),
        out_specs=(
            pl.BlockSpec(memory_space=pltpu.VMEM),
            pl.BlockSpec(memory_space=pltpu.VMEM),
        ),
        scratch_shapes=scratch,
        compiler_params=pltpu.CompilerParams(
            collective_id=0, has_side_effects=True, vmem_limit_bytes=60 * 1024 * 1024
        ),
        cost_estimate=pl.CostEstimate(
            flops=12_000_000_000, bytes_accessed=6_000_000, transcendentals=3_000_000
        ),
    )(*operands)
    mesh_out, grad = pl.pallas_call(
        widen,
        out_shape=(
            jax.ShapeDtypeStruct((1, NODES, D), BF),
            jax.ShapeDtypeStruct((D, D), F32),
        ),
        in_specs=[pl.BlockSpec(memory_space=pl.ANY)] * 2,
        out_specs=[pl.BlockSpec(memory_space=pl.ANY)] * 2,
        scratch_shapes=[
            vmem((D, D), BF),
            vmem((D, D), F32),
            vmem((NODES, D), BF),
            dma((5,)),
            dma((5,)),
        ],
    )(mesh_out, grad)
    return mesh_out, grad


def solution(mesh):
    in_specs = (
        P(None, "region"),
        P("noise", None, "region"),
        P("noise"),
        P("region", None, None),
        P("region"),
        P("region"),
        P(None, "region"),
        P("region", None),
        P("region", None),
        P(),
        P(),
        P(),
        P(),
        P(),
        P(),
        P(),
        P("noise", "region", None),
    )
    out_specs = (P("noise", "region", None), P())
    return jax.shard_map(body, mesh=mesh, in_specs=in_specs, out_specs=out_specs, check_vma=False)
```

```python
import math

import jax
import jax.numpy as jnp
from jax import lax
from jax.experimental import pallas as pl
from jax.experimental.pallas import tpu as pltpu
from jax.sharding import PartitionSpec as P

BF = jnp.bfloat16
F32 = jnp.float32

D = 512
HEADS = 4
HEAD = 128
VARS = 84
VPAD = 96
GEO = 4
PLAN = 20
K_NB = 32
HALO = 128
NODES = 256
GRID = 2048
EDGES = 4096
SLOT = 128
REGIONS = 32
PLANES = 8
ROWS = 4
XS = 4
ETILE = 512
HSPLIT = 1
PIECE = 32
HALF = GRID // 2
KCAT = 128

sigma_max = 80.0
sigma_min = 0.03
plan_rho = 7.0
norm_eps = 1e-05
head_eps = 1e-06

UP_ROOT = sigma_max ** (1.0 / plan_rho)
LOW_ROOT = sigma_min ** (1.0 / plan_rho)

AROUND = sorted(
    [(dx, dy) for dx in range(XS) for dy in range(ROWS) if dx or dy],
    key=lambda d: (-min(d[0], XS - d[0]) - min(d[1], ROWS - d[1]), d),
)

COLUMN = sorted(
    [(dy, dz) for dy in range(ROWS) for dz in range(PLANES) if dy or dz],
    key=lambda d: (-min(d[0], ROWS - d[0]) - min(d[1], PLANES - d[1]), d),
)

NT = (((1,), (1,)), ((), ()))


def dot(a, b):
    return jnp.dot(a, b, preferred_element_type=F32)


def dot_nt(a, b):
    return lax.dot_general(a, b, NT, preferred_element_type=F32)


def one_hot(code_row, rows):
    n = code_row.shape[1]
    ids = lax.broadcasted_iota(jnp.int32, (rows, n), 0).astype(F32).astype(BF)
    want = jnp.broadcast_to(code_row, (rows, n))
    return jnp.where(ids == want, jnp.ones((), BF), jnp.zeros((), BF))


def lanes(ref, first, count):
    return jnp.concatenate([ref[pl.ds(first + k, 1), :] for k in range(count)], axis=1)


def rms(values, epsilon):
    return values * lax.rsqrt(jnp.mean(values * values, axis=-1, keepdims=True) + epsilon)


def units(projected):
    return [
        rms(projected[:, h * HEAD : (h + 1) * HEAD], head_eps).astype(BF) for h in range(HEADS)
    ]


def with_ones(values):
    return jnp.concatenate([values, jnp.ones(values.shape, BF)], axis=1)


def plane_offset(i):
    half = lax.div(i + 1, 2)
    return lax.rem(4 + half * (1 - 2 * lax.rem(i, 2)) + PLANES, PLANES)


def kernel(
    level_ref,
    send_hbm,
    esrc_hbm,
    edst_hbm,
    nb_hbm,
    target_hbm,
    noise_hbm,
    geom_hbm,
    mesh_hbm,
    gw_hbm,
    ew_hbm,
    mw_hbm,
    eg_hbm,
    ag_hbm,
    qkv_hbm,
    ow_hbm,
    cot_hbm,
    mesh_out_hbm,
    grad_hbm,
    send_v,
    esrc_v,
    edst_v,
    nb_v,
    target_v,
    noise_v,
    geom_v,
    mesh_v,
    gw_v,
    ew_v,
    mw_v,
    eg_v,
    ag_v,
    qkv_v,
    ow_v,
    cot_v,
    in_sem,
    g_v,
    sbuf,
    rbuf,
    code_v,
    jbit_v,
    dstf_v,
    wc_v,
    wt_v,
    tab_v,
    acc_v,
    node_v,
    hid_v,
    count_t,
    count_l,
    count_h,
    enc_v,
    nrm_v,
    halo_v,
    att_v,
    attt_v,
    a2a_send,
    a2a_recv,
    halo_send,
    halo_recv,
    p_v,
    sb1,
    rb1,
    sb2,
    rb2,
    zbuf,
    fbuf,
    mout_v,
    s1_send,
    s1_recv,
    s2_send,
    s2_recv,
    s3_send,
    s3_recv,
    g2_send,
    g2_recv,
    g1_send,
    g1_recv,
    out_sem,
):
    noise = lax.axis_index("noise")
    me = lax.axis_index("region")
    core = lax.rem(noise, 2)
    mx = lax.div(noise, 2)
    mz = lax.div(me, ROWS)
    my = lax.rem(me, ROWS)
    partner = noise + 1 - 2 * core
    region_next = lax.rem(me + 1, REGIONS)
    region_prev = lax.rem(me + REGIONS - 1, REGIONS)

    def across(dx, dy):
        return {
            "noise": lax.rem(mx + dx, XS) * 2 + core,
            "region": mz * ROWS + lax.rem(my + dy, ROWS),
        }

    def region_at(dy, dz):
        return lax.rem(mz + dz, PLANES) * ROWS + lax.rem(my + dy, ROWS)

    def piece(x, y):
        return pl.ds(pl.multiple_of((x * ROWS + y) * PIECE, PIECE), PIECE)

    pairs = [
        (noise_hbm.at[0], noise_v),
        (target_hbm, target_v),
        (send_hbm.at[0], send_v),
        (esrc_hbm, esrc_v),
        (edst_hbm, edst_v),
        (nb_hbm, nb_v),
        (geom_hbm, geom_v),
        (gw_hbm, gw_v),
        (ew_hbm, ew_v),
        (mw_hbm, mw_v),
        (mesh_hbm, mesh_v),
        (eg_hbm, eg_v),
        (ag_hbm, ag_v),
        (qkv_hbm, qkv_v),
        (cot_hbm.at[0], cot_v),
        (ow_hbm, ow_v),
    ]
    loads = [pltpu.make_async_copy(s, d, in_sem.at[i]) for i, (s, d) in enumerate(pairs)]
    (
        ld_noise,
        ld_target,
        ld_send,
        ld_esrc,
        ld_edst,
        ld_nb,
        ld_geom,
        ld_gw,
        ld_ew,
        ld_mw,
        ld_mesh,
        ld_eg,
        ld_ag,
        ld_qkv,
        ld_cot,
        ld_ow,
    ) = loads
    for load in loads[:3]:
        load.start()

    barrier = pltpu.get_barrier_semaphore()

    def tell(device):
        pl.semaphore_signal(
            barrier, inc=1, device_id=device, device_id_type=pl.DeviceIdType.MESH
        )

    for dy, dz in COLUMN:
        tell({"region": region_at(dy, dz)})
    beyond = [(dx, dy) for dx, dy in AROUND if dx]
    for dx, dy in beyond:
        tell(across(dx, dy))
    tell({"noise": partner})
    for load in loads[3:]:
        load.start()

    g_v[80:96, :] = jnp.zeros((16, HALF), BF)
    g_v[176:192, :] = jnp.zeros((16, HALF), BF)
    level = jnp.broadcast_to(level_ref[...], (1, HALF)).astype(F32) * (1.0 / (PLAN - 1))
    root = UP_ROOT + level * (LOW_ROOT - UP_ROOT)
    root2 = root * root
    sigma = root2 * root2 * root2 * root
    scale = lax.rsqrt(1.0 + sigma * sigma)
    ld_noise.wait()
    ld_target.wait()
    for part in range(2):
        cols = slice(part * HALF, (part + 1) * HALF)
        noised = (
            target_v[:, cols].astype(F32) + sigma * noise_v[:, cols].astype(F32)
        ) * scale
        g_v[part * VPAD : part * VPAD + VARS, :] = noised.astype(BF)
    ld_send.wait()
    def pick_plane(z):
        idx = lanes(send_v, ROWS * z, ROWS)
        upper = idx >= HALF
        low = jnp.where(upper, idx - HALF, idx).astype(F32)
        hot = jnp.concatenate(
            [one_hot((low - 256.0 * k).astype(BF), 256) for k in range(HALF // 256)], axis=0
        )
        both = dot(g_v[...], hot)
        picked = jnp.where(upper, both[VPAD:, :], both[:VPAD, :]).astype(BF)
        for k in range(ROWS):
            sbuf[ROWS * z + k] = picked[:VARS, k * SLOT : (k + 1) * SLOT]

    def copy_plane(z):
        for k in range(ROWS):
            r = ROWS * z + k

            @pl.when(r != me)
            def _():
                pltpu.make_async_remote_copy(
                    src_ref=sbuf.at[r],
                    dst_ref=rbuf.at[me],
                    send_sem=a2a_send,
                    recv_sem=a2a_recv.at[mz],
                    device_id={"region": r},
                    device_id_type=pl.DeviceIdType.MESH,
                ).start()

            @pl.when(r == me)
            def _():
                pltpu.make_async_copy(sbuf.at[r], rbuf.at[me], a2a_recv.at[mz]).start()

    def send_plane(i, carry):
        z = lax.rem(mz + plane_offset(i), PLANES)
        pick_plane(z)
        copy_plane(z)
        return carry

    with jax.named_scope("send_columns"):
        pick_plane(lax.rem(mz + 4, PLANES))
        pl.semaphore_wait(barrier, REGIONS - 1 + len(beyond) + 1)
        copy_plane(lax.rem(mz + 4, PLANES))
        lax.fori_loop(1, PLANES, send_plane, 0)

    with jax.named_scope("tables"):
        ld_esrc.wait()
        ld_edst.wait()
        src = esrc_v[...]
        code_v[...] = (
            (src >> 9) * 256 + ((src >> 8) & 1) * 128 + (src & 127)
        ).astype(F32)
        jbit_v[...] = (src >> 7) & 1
        dstf_v[...] = edst_v[...].astype(F32)
        acc_v[...] = jnp.zeros((KCAT, EDGES), BF)
        tab_v[...] = jnp.zeros((2 * VPAD, 2 * SLOT), BF)
        ld_geom.wait()
        acc_v[VPAD : VPAD + GEO, :] = geom_v[...]
        ld_gw.wait()
        ld_ew.wait()
        wc_v[...] = jnp.zeros((KCAT, D), F32)
        wc_v[0:VARS, :] = gw_v[...].astype(F32)
        wc_v[VPAD : VPAD + GEO, :] = ew_v[...].astype(F32)
        wt_v[...] = wc_v[...].T.astype(BF)
        for e in range(EDGES // ETILE):
            row = lanes(dstf_v, e * (ETILE // 128), ETILE // 128).astype(BF)
            node_v[:, e * ETILE : (e + 1) * ETILE] = one_hot(row, NODES)
        ld_nb.wait()
        local = nb_v[...] - me * NODES + HALO
        local = jnp.where(local < 0, local + NODES * REGIONS, local)
        local = jnp.where(local >= NODES * REGIONS, local - NODES * REGIONS, local)
        for block in range(2 * NODES // 64):
            ids = lax.broadcasted_iota(jnp.int32, (64, NODES), 0) + block * 64
            total = jnp.zeros((64, NODES), F32)
            for j in range(K_NB):
                total = total + jnp.where(ids == local[j : j + 1, :], 1.0, 0.0)
            spot = slice(block * 64, (block + 1) * 64)
            count_t[spot, :] = total
        count_l[...] = count_t[HALO : HALO + NODES, :].T
        count_h[:, :HALO] = count_t[:HALO, :].T
        count_h[:, HALO:] = count_t[HALO + NODES :, :].T

    def gather_plane(i, carry):
        z = lax.rem(mz + PLANES - plane_offset(i), PLANES)
        window = rbuf.at[pl.ds(ROWS * z, ROWS)]
        pltpu.make_async_copy(window, window, a2a_recv.at[z]).wait()
        for k in range(ROWS):
            top, left = (k % 2) * VPAD, (k // 2) * SLOT
            tab_v[top : top + VARS, left : left + SLOT] = rbuf[ROWS * z + k]
        table = tab_v[...]
        base = (z * 256).astype(F32)
        for e in range(EDGES // ETILE):
            first = e * (ETILE // 128)
            cols = slice(e * ETILE, (e + 1) * ETILE)
            hot = one_hot((lanes(code_v, first, ETILE // 128) - base).astype(BF), 256)
            both = dot(table, hot)
            odd = lanes(jbit_v, first, ETILE // 128) == 1
            picked = jnp.where(odd, both[VPAD:, :], both[:VPAD, :]).astype(BF)
            acc_v[0:VPAD, cols] = acc_v[0:VPAD, cols] + picked
        return carry

    with jax.named_scope("gather_edges"):
        lax.fori_loop(0, PLANES, gather_plane, 0)

    with jax.named_scope("hidden"):
        for e in range(EDGES // ETILE):
            cols = slice(e * ETILE, (e + 1) * ETILE)
            x = dot(wt_v[...], acc_v[:, cols])
            half = (0.5 * x).astype(BF)
            hid_v[:, cols] = half + half * jnp.tanh(half)
        hidden_sum = dot_nt(node_v[...], hid_v[...])

    with jax.named_scope("encode"):
        ld_mw.wait()
        ld_mesh.wait()
        ld_eg.wait()
        ld_ag.wait()
        high = hidden_sum.astype(BF)
        rest = (hidden_sum - high.astype(F32)).astype(BF)
        aggregate = dot(high, mw_v[...]) + dot(rest, mw_v[...])
        encoded = mesh_v[...].astype(F32) + rms(aggregate, norm_eps) * eg_v[...]
        enc_v[...] = encoded
        nrm_v[...] = (rms(encoded, norm_eps) * ag_v[...]).astype(BF)

    step = HALO // HSPLIT
    for part in range(HSPLIT):
        for side, first, there, to in (
            (0, 0, HALO, region_prev),
            (1, NODES - HALO, 0, region_next),
        ):
            pltpu.make_async_remote_copy(
                src_ref=nrm_v.at[first + part * step : first + (part + 1) * step],
                dst_ref=halo_v.at[there + part * step : there + (part + 1) * step],
                send_sem=halo_send,
                recv_sem=halo_recv,
                device_id={"region": to},
                device_id_type=pl.DeviceIdType.MESH,
            ).start()
    halo_sent = pltpu.make_async_copy(nrm_v, nrm_v, halo_send)
    halo_got = pltpu.make_async_copy(halo_v, halo_v, halo_recv)

    with jax.named_scope("attention_local"):
        ld_qkv.wait()
        projected = dot(nrm_v[...], qkv_v[...])
        query = units(projected[:, :D])
        key = units(projected[:, D : 2 * D])
        value = projected[:, 2 * D :].astype(BF)
        rate = 1.0 / math.sqrt(HEAD)

        def mix(q, k, v, count):
            weight = (jnp.exp(dot_nt(q, k) * rate) * count).astype(BF)
            return dot(weight, with_ones(v))

        mixed = [
            mix(query[h], key[h], value[:, h * HEAD : (h + 1) * HEAD], count_l[...])
            for h in range(HEADS)
        ]

    other = pl.ds(pl.multiple_of((1 - core) * NODES, NODES), NODES)
    mine = pl.ds(pl.multiple_of(core * NODES, NODES), NODES)
    swaps = []
    with jax.named_scope("attention_halo"):
        halo_got.wait()
        ld_cot.wait()
        for pair in range(2):
            wide = 2 * HEAD
            beside = dot(halo_v[...], qkv_v[:, D + pair * wide : D + (pair + 1) * wide])
            value = dot(
                halo_v[...], qkv_v[:, 2 * D + pair * wide : 2 * D + (pair + 1) * wide]
            ).astype(BF)
            for h in range(2):
                head = 2 * pair + h
                cols = slice(h * HEAD, (h + 1) * HEAD)
                key = rms(beside[:, cols], head_eps).astype(BF)
                both = mixed[head] + mix(query[head], key, value[:, cols], count_h[...])
                att_v[:, head * HEAD : (head + 1) * HEAD] = both[:, :HEAD] / both[:, HEAD:]
            rows = slice(pair * wide, (pair + 1) * wide)
            attt_v[rows, :] = att_v[:, rows].T.astype(BF)
            sb1[rows, :] = dot(attt_v[rows, :], cot_v[:, other]).astype(BF)
            swap = pltpu.make_async_remote_copy(
                src_ref=sb1.at[rows],
                dst_ref=rb1.at[rows],
                send_sem=s1_send.at[pair],
                recv_sem=s1_recv.at[pair],
                device_id={"noise": partner},
                device_id_type=pl.DeviceIdType.MESH,
            )
            swap.start()
            swaps.append(swap)
            p_v[rows, :] = dot(attt_v[rows, :], cot_v[:, mine])

    with jax.named_scope("reduce_xy"):
        for pair in range(2):
            swaps[pair].wait_recv()
            rows = slice(pair * 2 * HEAD, (pair + 1) * 2 * HEAD)
            total = p_v[rows, :] + rb1[rows, :].astype(F32)
            p_v[rows, :] = total
            sb2[rows, :] = total.astype(BF)
            for x in (2 * pair, 2 * pair + 1):
                for dy in (2, 1, 3, 0):

                    @pl.when((x != mx) | (dy != 0))
                    def _():
                        slot = lax.rem(mx + XS - x, XS) * ROWS + (ROWS - dy) % ROWS - 1
                        pltpu.make_async_remote_copy(
                            src_ref=sb2.at[piece(x, lax.rem(my + dy, ROWS))],
                            dst_ref=rb2.at[slot],
                            send_sem=s2_send,
                            recv_sem=s2_recv,
                            device_id={
                                "noise": x * 2 + core,
                                "region": mz * ROWS + lax.rem(my + dy, ROWS),
                            },
                            device_id_type=pl.DeviceIdType.MESH,
                        ).start()

    with jax.named_scope("mesh_out"):
        ld_ow.wait()
        mout_v[...] = (enc_v[...] + dot(att_v[...].astype(BF), ow_v[...])).astype(BF)
        mesh_out = pltpu.make_async_copy(mout_v, mesh_out_hbm, out_sem.at[2 * XS])
        mesh_out.start()

    with jax.named_scope("reduce_z"):
        pltpu.make_async_copy(rb2, rb2, s2_recv).wait()
        total = p_v[piece(mx, my), :]
        for i in range(len(AROUND)):
            total = total + rb2[i].astype(F32)
        zbuf[mz] = total.astype(BF)
        for d in (4, 3, 5, 2, 6, 1, 7):
            pltpu.make_async_remote_copy(
                src_ref=zbuf.at[mz],
                dst_ref=zbuf.at[mz],
                send_sem=s3_send,
                recv_sem=s3_recv,
                device_id={"region": lax.rem(me + ROWS * d, REGIONS)},
                device_id_type=pl.DeviceIdType.MESH,
            ).start()
        seven = zbuf.at[0 : PLANES - 1]
        pltpu.make_async_copy(seven, seven, s3_recv).wait()
        total = zbuf[0].astype(F32)
        for z in range(1, PLANES):
            total = total + zbuf[z].astype(F32)

    with jax.named_scope("gather_xy"):
        place = piece(mx, my)
        fbuf[core, place, :] = total.astype(BF)
        for dx, dy in AROUND:
            pltpu.make_async_remote_copy(
                src_ref=fbuf.at[core, place],
                dst_ref=fbuf.at[core, place],
                send_sem=g2_send,
                recv_sem=g2_recv.at[dx],
                device_id=across(dx, dy),
                device_id_type=pl.DeviceIdType.MESH,
            ).start()

    with jax.named_scope("gather_core"):
        backs, outs = [], []
        for i, dx in enumerate((0, 1, 3, 2)):
            some = rb2.at[0 : ROWS - (dx == 0)]
            pltpu.make_async_copy(some, some, g2_recv.at[dx]).wait()
            rows = pl.ds(
                pl.multiple_of(lax.rem(mx + XS - dx, XS) * ROWS * PIECE, ROWS * PIECE),
                ROWS * PIECE,
            )
            back = pltpu.make_async_remote_copy(
                src_ref=fbuf.at[core, rows],
                dst_ref=fbuf.at[core, rows],
                send_sem=g1_send.at[i],
                recv_sem=g1_recv.at[i],
                device_id={"noise": partner},
                device_id_type=pl.DeviceIdType.MESH,
            )
            back.start()
            backs.append(back)
            out = pltpu.make_async_copy(
                fbuf.at[core, rows], grad_hbm.at[core, rows], out_sem.at[i]
            )
            out.start()
            outs.append((rows, out))
        for i in range(XS):
            backs[i].wait_recv()
            rows, out = outs[i]
            out = pltpu.make_async_copy(
                fbuf.at[1 - core, rows], grad_hbm.at[1 - core, rows], out_sem.at[XS + i]
            )
            out.start()
            outs.append((rows, out))

    sent = sbuf.at[0 : REGIONS - 1]
    pltpu.make_async_copy(sent, sent, a2a_send).wait()
    halo_sent.wait()
    for swap in swaps:
        swap.wait_send()
    pltpu.make_async_copy(rb2, rb2, s2_send).wait()
    pltpu.make_async_copy(seven, seven, s3_send).wait()
    pltpu.make_async_copy(rb2, rb2, g2_send).wait()
    mesh_out.wait()
    for back in backs:
        back.wait_send()
    for _, out in outs:
        out.wait()


def widen(mesh_hbm, grad_hbm, mesh_out_hbm, grad_out_hbm, narrow, wide, mesh_v, in_sems, out_sems):
    parts = [(c, slice(i * 128, (i + 1) * 128)) for i in range(4) for c in range(2)]
    got = [
        pltpu.make_async_copy(grad_hbm.at[c, rows], narrow.at[c, rows], in_sems.at[i])
        for i, (c, rows) in enumerate(parts)
    ]
    mesh_got = pltpu.make_async_copy(mesh_hbm, mesh_v, in_sems.at[8])
    for copy in got:
        copy.start()
    mesh_got.start()
    sent = []
    for i, (c, rows) in enumerate(parts):
        got[i].wait()
        wide[rows, c * NODES : (c + 1) * NODES] = narrow[c, rows, :].astype(F32)
        if c == 1:
            copy = pltpu.make_async_copy(
                wide.at[rows], grad_out_hbm.at[rows], out_sems.at[i // 2]
            )
            copy.start()
            sent.append(copy)
    mesh_got.wait()
    copy = pltpu.make_async_copy(mesh_v, mesh_out_hbm.at[0], out_sems.at[4])
    copy.start()
    for copy in sent + [copy]:
        copy.wait()


def body(
    target_state,
    noise_field,
    level_index,
    send_rows,
    edge_src,
    edge_dst,
    edge_geom,
    mesh_init,
    neighbours,
    grid_weight,
    edge_weight,
    message_weight,
    enc_gain,
    att_gain,
    qkv_weight,
    out_weight,
    cotangent,
):
    operands = (
        level_index.reshape(1, 1),
        send_rows,
        edge_src.reshape(EDGES // 128, 128),
        edge_dst.reshape(EDGES // 128, 128),
        neighbours.T,
        target_state,
        noise_field,
        edge_geom,
        mesh_init,
        grid_weight,
        edge_weight,
        message_weight,
        enc_gain.reshape(1, D),
        att_gain.reshape(1, D),
        qkv_weight,
        out_weight,
        cotangent,
    )
    vmem = pltpu.VMEM
    dma = pltpu.SemaphoreType.DMA
    i32 = jnp.int32
    scratch = [
        vmem((REGIONS, SLOT), i32),
        vmem((EDGES // 128, 128), i32),
        vmem((EDGES // 128, 128), i32),
        vmem((K_NB, NODES), i32),
        vmem((VARS, GRID), BF),
        vmem((VARS, GRID), BF),
        vmem((GEO, EDGES), BF),
        vmem((NODES, D), BF),
        vmem((VARS, D), BF),
        vmem((GEO, D), BF),
        vmem((D, D), BF),
        vmem((1, D), F32),
        vmem((1, D), F32),
        vmem((D, 3 * D), BF),
        vmem((D, D), BF),
        vmem((NODES, D), BF),
        dma((16,)),
        vmem((2 * VPAD, HALF), BF),
        vmem((REGIONS, VARS, SLOT), BF),
        vmem((REGIONS, VARS, SLOT), BF),
        vmem((EDGES // 128, 128), F32),
        vmem((EDGES // 128, 128), i32),
        vmem((EDGES // 128, 128), F32),
        vmem((KCAT, D), F32),
        vmem((D, KCAT), BF),
        vmem((2 * VPAD, 2 * SLOT), BF),
        vmem((KCAT, EDGES), BF),
        vmem((NODES, EDGES), BF),
        vmem((D, EDGES), BF),
        vmem((2 * NODES, NODES), F32),
        vmem((NODES, NODES), F32),
        vmem((NODES, NODES), F32),
        vmem((NODES, D), F32),
        vmem((NODES, D), BF),
        vmem((2 * HALO, D), BF),
        vmem((NODES, D), F32),
        vmem((D, NODES), BF),
        dma,
        dma((PLANES,)),
        dma,
        dma,
        vmem((D, NODES), F32),
        vmem((D, NODES), BF),
        vmem((D, NODES), BF),
        vmem((D, NODES), BF),
        vmem((len(AROUND), PIECE, NODES), BF),
        vmem((PLANES, PIECE, NODES), BF),
        vmem((2, D, NODES), BF),
        vmem((NODES, D), BF),
        dma((2,)),
        dma((2,)),
    ] + [dma] * 5 + [dma((XS,))] * 3 + [dma((2 * XS + 1,))]
    mesh_out, grad = pl.pallas_call(
        kernel,
        out_shape=(
            jax.ShapeDtypeStruct((NODES, D), BF),
            jax.ShapeDtypeStruct((2, D, NODES), BF),
        ),
        in_specs=[pl.BlockSpec(memory_space=pltpu.VMEM)]
        + [pl.BlockSpec(memory_space=pl.ANY)] * (len(operands) - 1),
        out_specs=[pl.BlockSpec(memory_space=pl.ANY)] * 2,
        scratch_shapes=scratch,
        compiler_params=pltpu.CompilerParams(
            collective_id=0, has_side_effects=True, vmem_limit_bytes=60 * 1024 * 1024
        ),
        cost_estimate=pl.CostEstimate(
            flops=12_000_000_000, bytes_accessed=6_000_000, transcendentals=3_000_000
        ),
    )(*operands)
    mesh_out, grad = pl.pallas_call(
        widen,
        out_shape=(
            jax.ShapeDtypeStruct((1, NODES, D), BF),
            jax.ShapeDtypeStruct((D, D), F32),
        ),
        in_specs=[pl.BlockSpec(memory_space=pl.ANY)] * 2,
        out_specs=[pl.BlockSpec(memory_space=pl.ANY)] * 2,
        scratch_shapes=[
            vmem((2, D, NODES), BF),
            vmem((D, D), F32),
            vmem((NODES, D), BF),
            dma((9,)),
            dma((5,)),
        ],
    )(mesh_out, grad)
    return mesh_out, grad


def solution(mesh):
    in_specs = (
        P(None, "region"),
        P("noise", None, "region"),
        P("noise"),
        P("region", None, None),
        P("region"),
        P("region"),
        P(None, "region"),
        P("region", None),
        P("region", None),
        P(),
        P(),
        P(),
        P(),
        P(),
        P(),
        P(),
        P("noise", "region", None),
    )
    out_specs = (P("noise", "region", None), P())
    return jax.shard_map(body, mesh=mesh, in_specs=in_specs, out_specs=out_specs, check_vma=False)
```

```python
import math

import jax
import jax.numpy as jnp
from jax import lax
from jax.experimental import pallas as pl
from jax.experimental.pallas import tpu as pltpu
from jax.sharding import PartitionSpec as P

BF = jnp.bfloat16
F32 = jnp.float32

D = 512
HEADS = 4
HEAD = 128
VARS = 84
VPAD = 96
GEO = 4
PLAN = 20
K_NB = 32
HALO = 128
NODES = 256
GRID = 2048
EDGES = 4096
SLOT = 128
REGIONS = 32
PLANES = 8
ROWS = 4
XS = 4
ETILE = 512
HSPLIT = 1
PIECE = 32
HALF = GRID // 2
KCAT = 128

sigma_max = 80.0
sigma_min = 0.03
plan_rho = 7.0
norm_eps = 1e-05
head_eps = 1e-06

UP_ROOT = sigma_max ** (1.0 / plan_rho)
LOW_ROOT = sigma_min ** (1.0 / plan_rho)

AROUND = sorted(
    [(dx, dy) for dx in range(XS) for dy in range(ROWS) if dx or dy],
    key=lambda d: (-min(d[0], XS - d[0]) - min(d[1], ROWS - d[1]), d),
)

COLUMN = sorted(
    [(dy, dz) for dy in range(ROWS) for dz in range(PLANES) if dy or dz],
    key=lambda d: (-min(d[0], ROWS - d[0]) - min(d[1], PLANES - d[1]), d),
)

NT = (((1,), (1,)), ((), ()))


def dot(a, b):
    return jnp.dot(a, b, preferred_element_type=F32)


def dot_nt(a, b):
    return lax.dot_general(a, b, NT, preferred_element_type=F32)


def one_hot(code_row, rows):
    n = code_row.shape[1]
    ids = lax.broadcasted_iota(jnp.int32, (rows, n), 0).astype(F32).astype(BF)
    want = jnp.broadcast_to(code_row, (rows, n))
    return jnp.where(ids == want, jnp.ones((), BF), jnp.zeros((), BF))


def lanes(ref, first, count):
    return jnp.concatenate([ref[pl.ds(first + k, 1), :] for k in range(count)], axis=1)


def rms(values, epsilon):
    return values * lax.rsqrt(jnp.mean(values * values, axis=-1, keepdims=True) + epsilon)


def units(projected):
    return [
        rms(projected[:, h * HEAD : (h + 1) * HEAD], head_eps).astype(BF) for h in range(HEADS)
    ]


def with_ones(values):
    return jnp.concatenate([values, jnp.ones(values.shape, BF)], axis=1)


def plane_offset(i):
    half = lax.div(i + 1, 2)
    return lax.rem(4 + half * (1 - 2 * lax.rem(i, 2)) + PLANES, PLANES)


def kernel(
    level_ref,
    send_hbm,
    esrc_hbm,
    edst_hbm,
    nb_hbm,
    target_hbm,
    noise_hbm,
    geom_hbm,
    mesh_hbm,
    gw_hbm,
    ew_hbm,
    mw_hbm,
    eg_hbm,
    ag_hbm,
    qkv_hbm,
    ow_hbm,
    cot_hbm,
    mesh_out_hbm,
    grad_hbm,
    send_v,
    esrc_v,
    edst_v,
    nb_v,
    target_v,
    noise_v,
    geom_v,
    mesh_v,
    gw_v,
    ew_v,
    mw_v,
    eg_v,
    ag_v,
    qkv_v,
    ow_v,
    cot_v,
    in_sem,
    g_v,
    sbuf,
    rbuf,
    code_v,
    jbit_v,
    dstf_v,
    wc_v,
    wt_v,
    tab_v,
    acc_v,
    node_v,
    hid_v,
    count_t,
    count_l,
    count_h,
    enc_v,
    nrm_v,
    halo_v,
    att_v,
    attt_v,
    a2a_send,
    a2a_recv,
    halo_send,
    halo_recv,
    p_v,
    sb1,
    rb1,
    sb2,
    rb2,
    zbuf,
    fbuf,
    mout_v,
    s1_send,
    s1_recv,
    s2_send,
    s2_recv,
    s3_send,
    s3_recv,
    g2_send,
    g2_recv,
    g1_send,
    g1_recv,
    out_sem,
):
    noise = lax.axis_index("noise")
    me = lax.axis_index("region")
    core = lax.rem(noise, 2)
    mx = lax.div(noise, 2)
    mz = lax.div(me, ROWS)
    my = lax.rem(me, ROWS)
    partner = noise + 1 - 2 * core
    region_next = lax.rem(me + 1, REGIONS)
    region_prev = lax.rem(me + REGIONS - 1, REGIONS)

    def across(dx, dy):
        return {
            "noise": lax.rem(mx + dx, XS) * 2 + core,
            "region": mz * ROWS + lax.rem(my + dy, ROWS),
        }

    def region_at(dy, dz):
        return lax.rem(mz + dz, PLANES) * ROWS + lax.rem(my + dy, ROWS)

    def sixteen(pair, x, y):
        return pl.ds(pl.multiple_of(pair * NODES + (x * ROWS + y) * 16, 16), 16)

    def piece(x, y):
        return pl.ds(pl.multiple_of((x * ROWS + y) * PIECE, PIECE), PIECE)

    pairs = [
        (noise_hbm.at[0], noise_v),
        (target_hbm, target_v),
        (send_hbm.at[0], send_v),
        (esrc_hbm, esrc_v),
        (edst_hbm, edst_v),
        (nb_hbm, nb_v),
        (geom_hbm, geom_v),
        (gw_hbm, gw_v),
        (ew_hbm, ew_v),
        (mw_hbm, mw_v),
        (mesh_hbm, mesh_v),
        (eg_hbm, eg_v),
        (ag_hbm, ag_v),
        (qkv_hbm, qkv_v),
        (cot_hbm.at[0], cot_v),
        (ow_hbm, ow_v),
    ]
    loads = [pltpu.make_async_copy(s, d, in_sem.at[i]) for i, (s, d) in enumerate(pairs)]
    (
        ld_noise,
        ld_target,
        ld_send,
        ld_esrc,
        ld_edst,
        ld_nb,
        ld_geom,
        ld_gw,
        ld_ew,
        ld_mw,
        ld_mesh,
        ld_eg,
        ld_ag,
        ld_qkv,
        ld_cot,
        ld_ow,
    ) = loads
    for load in loads[:3]:
        load.start()

    barrier = pltpu.get_barrier_semaphore()

    def tell(device):
        pl.semaphore_signal(
            barrier, inc=1, device_id=device, device_id_type=pl.DeviceIdType.MESH
        )

    for dy, dz in COLUMN:
        tell({"region": region_at(dy, dz)})
    beyond = [(dx, dy) for dx, dy in AROUND if dx]
    for dx, dy in beyond:
        tell(across(dx, dy))
    tell({"noise": partner})
    for load in loads[3:]:
        load.start()

    g_v[80:96, :] = jnp.zeros((16, HALF), BF)
    g_v[176:192, :] = jnp.zeros((16, HALF), BF)
    level = jnp.broadcast_to(level_ref[...], (1, HALF)).astype(F32) * (1.0 / (PLAN - 1))
    root = UP_ROOT + level * (LOW_ROOT - UP_ROOT)
    root2 = root * root
    sigma = root2 * root2 * root2 * root
    scale = lax.rsqrt(1.0 + sigma * sigma)
    ld_noise.wait()
    ld_target.wait()
    for part in range(2):
        cols = slice(part * HALF, (part + 1) * HALF)
        noised = (
            target_v[:, cols].astype(F32) + sigma * noise_v[:, cols].astype(F32)
        ) * scale
        g_v[part * VPAD : part * VPAD + VARS, :] = noised.astype(BF)
    ld_send.wait()
    def pick_plane(z):
        idx = lanes(send_v, ROWS * z, ROWS)
        upper = idx >= HALF
        low = jnp.where(upper, idx - HALF, idx).astype(F32)
        hot = jnp.concatenate(
            [one_hot((low - 256.0 * k).astype(BF), 256) for k in range(HALF // 256)], axis=0
        )
        both = dot(g_v[...], hot)
        picked = jnp.where(upper, both[VPAD:, :], both[:VPAD, :]).astype(BF)
        for k in range(ROWS):
            sbuf[ROWS * z + k] = picked[:VARS, k * SLOT : (k + 1) * SLOT]

    def copy_plane(z):
        for k, l in ((0, 3), (3, 0), (1, 2), (2, 1)):
            r = ROWS * z + jnp.where(lax.rem(z, 2) == 0, k, l)

            @pl.when(r != me)
            def _():
                pltpu.make_async_remote_copy(
                    src_ref=sbuf.at[r],
                    dst_ref=rbuf.at[me],
                    send_sem=a2a_send,
                    recv_sem=a2a_recv.at[mz],
                    device_id={"region": r},
                    device_id_type=pl.DeviceIdType.MESH,
                ).start()

            @pl.when(r == me)
            def _():
                pltpu.make_async_copy(sbuf.at[r], rbuf.at[me], a2a_recv.at[mz]).start()

    def send_plane(i, carry):
        z = lax.rem(mz + plane_offset(i), PLANES)
        pick_plane(z)
        copy_plane(z)
        return carry

    with jax.named_scope("send_columns"):
        pick_plane(lax.rem(mz + 4, PLANES))
        pl.semaphore_wait(barrier, REGIONS - 1 + len(beyond) + 1)
        copy_plane(lax.rem(mz + 4, PLANES))
        lax.fori_loop(1, PLANES, send_plane, 0)

    with jax.named_scope("tables"):
        ld_esrc.wait()
        ld_edst.wait()
        src = esrc_v[...]
        code_v[...] = (
            (src >> 9) * 256 + ((src >> 8) & 1) * 128 + (src & 127)
        ).astype(F32)
        jbit_v[...] = (src >> 7) & 1
        dstf_v[...] = edst_v[...].astype(F32)
        acc_v[...] = jnp.zeros((KCAT, EDGES), BF)
        tab_v[...] = jnp.zeros((2 * VPAD, 2 * SLOT), BF)
        ld_geom.wait()
        acc_v[VPAD : VPAD + GEO, :] = geom_v[...]
        ld_gw.wait()
        ld_ew.wait()
        wc_v[...] = jnp.zeros((KCAT, D), F32)
        wc_v[0:VARS, :] = gw_v[...].astype(F32)
        wc_v[VPAD : VPAD + GEO, :] = ew_v[...].astype(F32)
        wt_v[...] = wc_v[...].T.astype(BF)
        for e in range(EDGES // ETILE):
            row = lanes(dstf_v, e * (ETILE // 128), ETILE // 128).astype(BF)
            node_v[:, e * ETILE : (e + 1) * ETILE] = one_hot(row, NODES)
        ld_nb.wait()
        local = nb_v[...] - me * NODES + HALO
        local = jnp.where(local < 0, local + NODES * REGIONS, local)
        local = jnp.where(local >= NODES * REGIONS, local - NODES * REGIONS, local)
        for block in range(2 * NODES // 64):
            ids = lax.broadcasted_iota(jnp.int32, (64, NODES), 0) + block * 64
            total = jnp.zeros((64, NODES), F32)
            for j in range(K_NB):
                total = total + jnp.where(ids == local[j : j + 1, :], 1.0, 0.0)
            spot = slice(block * 64, (block + 1) * 64)
            count_t[spot, :] = total
        count_l[...] = count_t[HALO : HALO + NODES, :].T
        count_h[:, :HALO] = count_t[:HALO, :].T
        count_h[:, HALO:] = count_t[HALO + NODES :, :].T

    def gather_plane(i, carry):
        z = lax.rem(mz + PLANES - plane_offset(i), PLANES)
        window = rbuf.at[pl.ds(ROWS * z, ROWS)]
        pltpu.make_async_copy(window, window, a2a_recv.at[z]).wait()
        for k in range(ROWS):
            top, left = (k % 2) * VPAD, (k // 2) * SLOT
            tab_v[top : top + VARS, left : left + SLOT] = rbuf[ROWS * z + k]
        table = tab_v[...]
        base = (z * 256).astype(F32)
        for e in range(EDGES // ETILE):
            first = e * (ETILE // 128)
            cols = slice(e * ETILE, (e + 1) * ETILE)
            hot = one_hot((lanes(code_v, first, ETILE // 128) - base).astype(BF), 256)
            both = dot(table, hot)
            odd = lanes(jbit_v, first, ETILE // 128) == 1
            picked = jnp.where(odd, both[VPAD:, :], both[:VPAD, :]).astype(BF)
            acc_v[0:VPAD, cols] = acc_v[0:VPAD, cols] + picked
        return carry

    with jax.named_scope("gather_edges"):
        lax.fori_loop(0, PLANES, gather_plane, 0)

    with jax.named_scope("hidden"):
        for e in range(EDGES // ETILE):
            cols = slice(e * ETILE, (e + 1) * ETILE)
            x = dot(wt_v[...], acc_v[:, cols])
            half = (0.5 * x).astype(BF)
            hid_v[:, cols] = half + half * jnp.tanh(half)
        hidden_sum = dot_nt(node_v[...], hid_v[...])

    with jax.named_scope("encode"):
        ld_mw.wait()
        ld_mesh.wait()
        ld_eg.wait()
        ld_ag.wait()
        high = hidden_sum.astype(BF)
        rest = (hidden_sum - high.astype(F32)).astype(BF)
        aggregate = dot(high, mw_v[...]) + dot(rest, mw_v[...])
        encoded = mesh_v[...].astype(F32) + rms(aggregate, norm_eps) * eg_v[...]
        enc_v[...] = encoded
        nrm_v[...] = (rms(encoded, norm_eps) * ag_v[...]).astype(BF)

    step = HALO // HSPLIT
    for part in range(HSPLIT):
        for side, first, there, to in (
            (0, 0, HALO, region_prev),
            (1, NODES - HALO, 0, region_next),
        ):
            pltpu.make_async_remote_copy(
                src_ref=nrm_v.at[first + part * step : first + (part + 1) * step],
                dst_ref=halo_v.at[there + part * step : there + (part + 1) * step],
                send_sem=halo_send,
                recv_sem=halo_recv,
                device_id={"region": to},
                device_id_type=pl.DeviceIdType.MESH,
            ).start()
    halo_sent = pltpu.make_async_copy(nrm_v, nrm_v, halo_send)
    halo_got = pltpu.make_async_copy(halo_v, halo_v, halo_recv)

    with jax.named_scope("attention_local"):
        ld_qkv.wait()
        projected = dot(nrm_v[...], qkv_v[...])
        query = units(projected[:, :D])
        key = units(projected[:, D : 2 * D])
        value = projected[:, 2 * D :].astype(BF)
        rate = 1.0 / math.sqrt(HEAD)

        def mix(q, k, v, count):
            weight = (jnp.exp(dot_nt(q, k) * rate) * count).astype(BF)
            return dot(weight, with_ones(v))

        mixed = [
            mix(query[h], key[h], value[:, h * HEAD : (h + 1) * HEAD], count_l[...])
            for h in range(HEADS)
        ]

    other = pl.ds(pl.multiple_of((1 - core) * NODES, NODES), NODES)
    mine = pl.ds(pl.multiple_of(core * NODES, NODES), NODES)
    swaps = []

    def send_pieces(pair):
        swaps[pair].wait_recv()
        rows = slice(pair * 2 * HEAD, (pair + 1) * 2 * HEAD)
        total = p_v[rows, :] + rb1[rows, :].astype(F32)
        p_v[rows, :] = total
        sb2[rows, :] = total.astype(BF)
        for i, (dx, dy) in enumerate(AROUND):
            there = sixteen(pair, lax.rem(mx + dx, XS), lax.rem(my + dy, ROWS))
            pltpu.make_async_remote_copy(
                src_ref=sb2.at[there],
                dst_ref=rb2.at[i, pair * 16 : (pair + 1) * 16],
                send_sem=s2_send,
                recv_sem=s2_recv,
                device_id=across(dx, dy),
                device_id_type=pl.DeviceIdType.MESH,
            ).start()

    with jax.named_scope("attention_halo"):
        halo_got.wait()
        ld_cot.wait()
        for pair in range(2):
            wide = 2 * HEAD
            beside = dot(halo_v[...], qkv_v[:, D + pair * wide : D + (pair + 1) * wide])
            value = dot(
                halo_v[...], qkv_v[:, 2 * D + pair * wide : 2 * D + (pair + 1) * wide]
            ).astype(BF)
            for h in range(2):
                head = 2 * pair + h
                cols = slice(h * HEAD, (h + 1) * HEAD)
                key = rms(beside[:, cols], head_eps).astype(BF)
                both = mixed[head] + mix(query[head], key, value[:, cols], count_h[...])
                att_v[:, head * HEAD : (head + 1) * HEAD] = both[:, :HEAD] / both[:, HEAD:]
            if pair == 1:
                send_pieces(0)
            rows = slice(pair * wide, (pair + 1) * wide)
            attt_v[rows, :] = att_v[:, rows].T.astype(BF)
            sb1[rows, :] = dot(attt_v[rows, :], cot_v[:, other]).astype(BF)
            swap = pltpu.make_async_remote_copy(
                src_ref=sb1.at[rows],
                dst_ref=rb1.at[rows],
                send_sem=s1_send.at[pair],
                recv_sem=s1_recv.at[pair],
                device_id={"noise": partner},
                device_id_type=pl.DeviceIdType.MESH,
            )
            swap.start()
            swaps.append(swap)
            p_v[rows, :] = dot(attt_v[rows, :], cot_v[:, mine])

    with jax.named_scope("reduce_xy"):
        send_pieces(1)

    with jax.named_scope("mesh_out"):
        ld_ow.wait()
        mout_v[...] = (enc_v[...] + dot(att_v[...].astype(BF), ow_v[...])).astype(BF)
        mesh_out = pltpu.make_async_copy(mout_v, mesh_out_hbm, out_sem.at[2 * XS])
        mesh_out.start()

    with jax.named_scope("reduce_z"):
        pltpu.make_async_copy(rb2, rb2, s2_recv).wait()
        total = jnp.concatenate([p_v[sixteen(pair, mx, my), :] for pair in range(2)], axis=0)
        for i in range(len(AROUND)):
            total = total + rb2[i].astype(F32)
        zbuf[mz] = total.astype(BF)
        for d in (4, 3, 5, 2, 6, 1, 7):
            pltpu.make_async_remote_copy(
                src_ref=zbuf.at[mz],
                dst_ref=zbuf.at[mz],
                send_sem=s3_send,
                recv_sem=s3_recv,
                device_id={"region": lax.rem(me + ROWS * d, REGIONS)},
                device_id_type=pl.DeviceIdType.MESH,
            ).start()
        seven = zbuf.at[0 : PLANES - 1]
        pltpu.make_async_copy(seven, seven, s3_recv).wait()
        total = zbuf[0].astype(F32)
        for z in range(1, PLANES):
            total = total + zbuf[z].astype(F32)

    with jax.named_scope("gather_xy"):
        place = piece(mx, my)
        fbuf[core, place, :] = total.astype(BF)
        for dx, dy in AROUND:
            pltpu.make_async_remote_copy(
                src_ref=fbuf.at[core, place],
                dst_ref=fbuf.at[core, place],
                send_sem=g2_send,
                recv_sem=g2_recv.at[dx],
                device_id=across(dx, dy),
                device_id_type=pl.DeviceIdType.MESH,
            ).start()

    with jax.named_scope("gather_core"):
        backs, outs = [], []
        for i, dx in enumerate((0, 1, 3, 2)):
            some = rb2.at[0 : ROWS - (dx == 0)]
            pltpu.make_async_copy(some, some, g2_recv.at[dx]).wait()
            rows = pl.ds(
                pl.multiple_of(lax.rem(mx + XS - dx, XS) * ROWS * PIECE, ROWS * PIECE),
                ROWS * PIECE,
            )
            back = pltpu.make_async_remote_copy(
                src_ref=fbuf.at[core, rows],
                dst_ref=fbuf.at[core, rows],
                send_sem=g1_send.at[i],
                recv_sem=g1_recv.at[i],
                device_id={"noise": partner},
                device_id_type=pl.DeviceIdType.MESH,
            )
            back.start()
            backs.append(back)
            out = pltpu.make_async_copy(
                fbuf.at[core, rows], grad_hbm.at[core, rows], out_sem.at[i]
            )
            out.start()
            outs.append((rows, out))
        for i in range(XS):
            backs[i].wait_recv()
            rows, out = outs[i]
            out = pltpu.make_async_copy(
                fbuf.at[1 - core, rows], grad_hbm.at[1 - core, rows], out_sem.at[XS + i]
            )
            out.start()
            outs.append((rows, out))

    sent = sbuf.at[0 : REGIONS - 1]
    pltpu.make_async_copy(sent, sent, a2a_send).wait()
    halo_sent.wait()
    for swap in swaps:
        swap.wait_send()
    pltpu.make_async_copy(rb2, rb2, s2_send).wait()
    pltpu.make_async_copy(seven, seven, s3_send).wait()
    pltpu.make_async_copy(rb2, rb2, g2_send).wait()
    mesh_out.wait()
    for back in backs:
        back.wait_send()
    for _, out in outs:
        out.wait()


def widen(mesh_hbm, grad_hbm, mesh_out_hbm, grad_out_hbm, narrow, wide, mesh_v, in_sems, out_sems):
    parts = [(c, slice(i * 128, (i + 1) * 128)) for i in range(4) for c in range(2)]
    got = [
        pltpu.make_async_copy(grad_hbm.at[c, rows], narrow.at[c, rows], in_sems.at[i])
        for i, (c, rows) in enumerate(parts)
    ]
    mesh_got = pltpu.make_async_copy(mesh_hbm, mesh_v, in_sems.at[8])
    for copy in got:
        copy.start()
    mesh_got.start()
    sent = []
    for i, (c, rows) in enumerate(parts):
        got[i].wait()
        for q in range(4):
            for pair in range(2):
                first = rows.start + q * PIECE + pair * 16
                to = pair * NODES + (rows.start // PIECE + q) * 16
                wide[to : to + 16, c * NODES : (c + 1) * NODES] = narrow[
                    c, first : first + 16, :
                ].astype(F32)
        if c == 1:
            for pair in range(2):
                block = pl.ds(pair * NODES + rows.start // 2, 64)
                copy = pltpu.make_async_copy(
                    wide.at[block], grad_out_hbm.at[block], out_sems.at[i - 1 + pair]
                )
                copy.start()
                sent.append(copy)
    mesh_got.wait()
    copy = pltpu.make_async_copy(mesh_v, mesh_out_hbm.at[0], out_sems.at[8])
    copy.start()
    for copy in sent + [copy]:
        copy.wait()


def body(
    target_state,
    noise_field,
    level_index,
    send_rows,
    edge_src,
    edge_dst,
    edge_geom,
    mesh_init,
    neighbours,
    grid_weight,
    edge_weight,
    message_weight,
    enc_gain,
    att_gain,
    qkv_weight,
    out_weight,
    cotangent,
):
    operands = (
        level_index.reshape(1, 1),
        send_rows,
        edge_src.reshape(EDGES // 128, 128),
        edge_dst.reshape(EDGES // 128, 128),
        neighbours.T,
        target_state,
        noise_field,
        edge_geom,
        mesh_init,
        grid_weight,
        edge_weight,
        message_weight,
        enc_gain.reshape(1, D),
        att_gain.reshape(1, D),
        qkv_weight,
        out_weight,
        cotangent,
    )
    vmem = pltpu.VMEM
    dma = pltpu.SemaphoreType.DMA
    i32 = jnp.int32
    scratch = [
        vmem((REGIONS, SLOT), i32),
        vmem((EDGES // 128, 128), i32),
        vmem((EDGES // 128, 128), i32),
        vmem((K_NB, NODES), i32),
        vmem((VARS, GRID), BF),
        vmem((VARS, GRID), BF),
        vmem((GEO, EDGES), BF),
        vmem((NODES, D), BF),
        vmem((VARS, D), BF),
        vmem((GEO, D), BF),
        vmem((D, D), BF),
        vmem((1, D), F32),
        vmem((1, D), F32),
        vmem((D, 3 * D), BF),
        vmem((D, D), BF),
        vmem((NODES, D), BF),
        dma((16,)),
        vmem((2 * VPAD, HALF), BF),
        vmem((REGIONS, VARS, SLOT), BF),
        vmem((REGIONS, VARS, SLOT), BF),
        vmem((EDGES // 128, 128), F32),
        vmem((EDGES // 128, 128), i32),
        vmem((EDGES // 128, 128), F32),
        vmem((KCAT, D), F32),
        vmem((D, KCAT), BF),
        vmem((2 * VPAD, 2 * SLOT), BF),
        vmem((KCAT, EDGES), BF),
        vmem((NODES, EDGES), BF),
        vmem((D, EDGES), BF),
        vmem((2 * NODES, NODES), F32),
        vmem((NODES, NODES), F32),
        vmem((NODES, NODES), F32),
        vmem((NODES, D), F32),
        vmem((NODES, D), BF),
        vmem((2 * HALO, D), BF),
        vmem((NODES, D), F32),
        vmem((D, NODES), BF),
        dma,
        dma((PLANES,)),
        dma,
        dma,
        vmem((D, NODES), F32),
        vmem((D, NODES), BF),
        vmem((D, NODES), BF),
        vmem((D, NODES), BF),
        vmem((len(AROUND), PIECE, NODES), BF),
        vmem((PLANES, PIECE, NODES), BF),
        vmem((2, D, NODES), BF),
        vmem((NODES, D), BF),
        dma((2,)),
        dma((2,)),
    ] + [dma] * 5 + [dma((XS,))] * 3 + [dma((2 * XS + 1,))]
    mesh_out, grad = pl.pallas_call(
        kernel,
        out_shape=(
            jax.ShapeDtypeStruct((NODES, D), BF),
            jax.ShapeDtypeStruct((2, D, NODES), BF),
        ),
        in_specs=[pl.BlockSpec(memory_space=pltpu.VMEM)]
        + [pl.BlockSpec(memory_space=pl.ANY)] * (len(operands) - 1),
        out_specs=[pl.BlockSpec(memory_space=pl.ANY)] * 2,
        scratch_shapes=scratch,
        compiler_params=pltpu.CompilerParams(
            collective_id=0, has_side_effects=True, vmem_limit_bytes=60 * 1024 * 1024
        ),
        cost_estimate=pl.CostEstimate(
            flops=12_000_000_000, bytes_accessed=6_000_000, transcendentals=3_000_000
        ),
    )(*operands)
    mesh_out, grad = pl.pallas_call(
        widen,
        out_shape=(
            jax.ShapeDtypeStruct((1, NODES, D), BF),
            jax.ShapeDtypeStruct((D, D), F32),
        ),
        in_specs=[pl.BlockSpec(memory_space=pl.ANY)] * 2,
        out_specs=[pl.BlockSpec(memory_space=pl.ANY)] * 2,
        scratch_shapes=[
            vmem((2, D, NODES), BF),
            vmem((D, D), F32),
            vmem((NODES, D), BF),
            dma((9,)),
            dma((9,)),
        ],
    )(mesh_out, grad)
    return mesh_out, grad


def solution(mesh):
    in_specs = (
        P(None, "region"),
        P("noise", None, "region"),
        P("noise"),
        P("region", None, None),
        P("region"),
        P("region"),
        P(None, "region"),
        P("region", None),
        P("region", None),
        P(),
        P(),
        P(),
        P(),
        P(),
        P(),
        P(),
        P("noise", "region", None),
    )
    out_specs = (P("noise", "region", None), P())
    return jax.shard_map(body, mesh=mesh, in_specs=in_specs, out_specs=out_specs, check_vma=False)
```

```python
import math

import jax
import jax.numpy as jnp
from jax import lax
from jax.experimental import pallas as pl
from jax.experimental.pallas import tpu as pltpu
from jax.sharding import PartitionSpec as P

BF = jnp.bfloat16
F32 = jnp.float32

D = 512
HEADS = 4
HEAD = 128
VARS = 84
VPAD = 96
GEO = 4
PLAN = 20
K_NB = 32
HALO = 128
NODES = 256
GRID = 2048
EDGES = 4096
SLOT = 128
REGIONS = 32
PLANES = 8
ROWS = 4
XS = 4
ETILE = 512
HSPLIT = 1
PIECE = 32
HALF = GRID // 2
KCAT = 128

sigma_max = 80.0
sigma_min = 0.03
plan_rho = 7.0
norm_eps = 1e-05
head_eps = 1e-06

UP_ROOT = sigma_max ** (1.0 / plan_rho)
LOW_ROOT = sigma_min ** (1.0 / plan_rho)

AROUND = sorted(
    [(dx, dy) for dx in range(XS) for dy in range(ROWS) if dx or dy],
    key=lambda d: (-min(d[0], XS - d[0]) - min(d[1], ROWS - d[1]), d),
)

COLUMN = sorted(
    [(dy, dz) for dy in range(ROWS) for dz in range(PLANES) if dy or dz],
    key=lambda d: (-min(d[0], ROWS - d[0]) - min(d[1], PLANES - d[1]), d),
)

NT = (((1,), (1,)), ((), ()))


def dot(a, b):
    return jnp.dot(a, b, preferred_element_type=F32)


def dot_nt(a, b):
    return lax.dot_general(a, b, NT, preferred_element_type=F32)


def one_hot(code_row, rows):
    n = code_row.shape[1]
    ids = lax.broadcasted_iota(jnp.int32, (rows, n), 0).astype(F32).astype(BF)
    want = jnp.broadcast_to(code_row, (rows, n))
    return jnp.where(ids == want, jnp.ones((), BF), jnp.zeros((), BF))


def lanes(ref, first, count):
    return jnp.concatenate([ref[pl.ds(first + k, 1), :] for k in range(count)], axis=1)


def rms(values, epsilon):
    return values * lax.rsqrt(jnp.mean(values * values, axis=-1, keepdims=True) + epsilon)


def units(projected):
    return [
        rms(projected[:, h * HEAD : (h + 1) * HEAD], head_eps).astype(BF) for h in range(HEADS)
    ]


def with_ones(values):
    return jnp.concatenate([values, jnp.ones(values.shape, BF)], axis=1)


def plane_offset(i):
    half = lax.div(i, 2) + 1
    return jnp.where(
        i == PLANES - 1, 0, jnp.where(lax.rem(i, 2) == 0, half, PLANES - half)
    )


def kernel(
    level_ref,
    send_hbm,
    esrc_hbm,
    edst_hbm,
    nb_hbm,
    target_hbm,
    noise_hbm,
    geom_hbm,
    mesh_hbm,
    gw_hbm,
    ew_hbm,
    mw_hbm,
    eg_hbm,
    ag_hbm,
    qkv_hbm,
    ow_hbm,
    cot_hbm,
    mesh_out_hbm,
    grad_hbm,
    send_v,
    esrc_v,
    edst_v,
    nb_v,
    target_v,
    noise_v,
    geom_v,
    mesh_v,
    gw_v,
    ew_v,
    mw_v,
    eg_v,
    ag_v,
    qkv_v,
    ow_v,
    cot_v,
    in_sem,
    g_v,
    sbuf,
    rbuf,
    code_v,
    jbit_v,
    dstf_v,
    wc_v,
    wt_v,
    tab_v,
    acc_v,
    node_v,
    hid_v,
    count_t,
    count_l,
    count_h,
    enc_v,
    nrm_v,
    halo_v,
    att_v,
    attt_v,
    a2a_send,
    a2a_recv,
    halo_send,
    halo_recv,
    p_v,
    sb1,
    rb1,
    sb2,
    rb2,
    zbuf,
    fbuf,
    mout_v,
    s1_send,
    s1_recv,
    s2_send,
    s2_recv,
    s3_send,
    s3_recv,
    g2_send,
    g2_recv,
    g1_send,
    g1_recv,
    out_sem,
):
    noise = lax.axis_index("noise")
    me = lax.axis_index("region")
    core = lax.rem(noise, 2)
    mx = lax.div(noise, 2)
    mz = lax.div(me, ROWS)
    my = lax.rem(me, ROWS)
    partner = noise + 1 - 2 * core
    region_next = lax.rem(me + 1, REGIONS)
    region_prev = lax.rem(me + REGIONS - 1, REGIONS)

    def across(dx, dy):
        return {
            "noise": lax.rem(mx + dx, XS) * 2 + core,
            "region": mz * ROWS + lax.rem(my + dy, ROWS),
        }

    def region_at(dy, dz):
        return lax.rem(mz + dz, PLANES) * ROWS + lax.rem(my + dy, ROWS)

    def sixteen(pair, x, y):
        return pl.ds(pl.multiple_of(pair * NODES + (x * ROWS + y) * 16, 16), 16)

    def piece(x, y):
        return pl.ds(pl.multiple_of((x * ROWS + y) * PIECE, PIECE), PIECE)

    pairs = [
        (noise_hbm.at[0], noise_v),
        (target_hbm, target_v),
        (send_hbm.at[0], send_v),
        (esrc_hbm, esrc_v),
        (edst_hbm, edst_v),
        (nb_hbm, nb_v),
        (geom_hbm, geom_v),
        (gw_hbm, gw_v),
        (ew_hbm, ew_v),
        (mw_hbm, mw_v),
        (mesh_hbm, mesh_v),
        (eg_hbm, eg_v),
        (ag_hbm, ag_v),
        (qkv_hbm, qkv_v),
        (cot_hbm.at[0], cot_v),
        (ow_hbm, ow_v),
    ]
    loads = [pltpu.make_async_copy(s, d, in_sem.at[i]) for i, (s, d) in enumerate(pairs)]
    (
        ld_noise,
        ld_target,
        ld_send,
        ld_esrc,
        ld_edst,
        ld_nb,
        ld_geom,
        ld_gw,
        ld_ew,
        ld_mw,
        ld_mesh,
        ld_eg,
        ld_ag,
        ld_qkv,
        ld_cot,
        ld_ow,
    ) = loads
    for load in loads[:3]:
        load.start()

    barrier = pltpu.get_barrier_semaphore()

    def tell(device):
        pl.semaphore_signal(
            barrier, inc=1, device_id=device, device_id_type=pl.DeviceIdType.MESH
        )

    for dy, dz in COLUMN:
        tell({"region": region_at(dy, dz)})
    beyond = [(dx, dy) for dx, dy in AROUND if dx]
    for dx, dy in beyond:
        tell(across(dx, dy))
    tell({"noise": partner})
    for load in loads[3:]:
        load.start()

    g_v[80:96, :] = jnp.zeros((16, HALF), BF)
    g_v[176:192, :] = jnp.zeros((16, HALF), BF)
    level = jnp.broadcast_to(level_ref[...], (1, HALF)).astype(F32) * (1.0 / (PLAN - 1))
    root = UP_ROOT + level * (LOW_ROOT - UP_ROOT)
    root2 = root * root
    sigma = root2 * root2 * root2 * root
    scale = lax.rsqrt(1.0 + sigma * sigma)
    ld_noise.wait()
    ld_target.wait()
    for part in range(2):
        cols = slice(part * HALF, (part + 1) * HALF)
        noised = (
            target_v[:, cols].astype(F32) + sigma * noise_v[:, cols].astype(F32)
        ) * scale
        g_v[part * VPAD : part * VPAD + VARS, :] = noised.astype(BF)
    ld_send.wait()
    def pick_plane(z):
        idx = lanes(send_v, ROWS * z, ROWS)
        upper = idx >= HALF
        low = jnp.where(upper, idx - HALF, idx).astype(F32)
        hot = jnp.concatenate(
            [one_hot((low - 256.0 * k).astype(BF), 256) for k in range(HALF // 256)], axis=0
        )
        both = dot(g_v[...], hot)
        picked = jnp.where(upper, both[VPAD:, :], both[:VPAD, :]).astype(BF)
        for k in range(ROWS):
            sbuf[ROWS * z + k] = picked[:VARS, k * SLOT : (k + 1) * SLOT]

    def copy_plane(z):
        for k, l in ((0, 3), (3, 0), (1, 2), (2, 1)):
            r = ROWS * z + jnp.where(lax.rem(z, 2) == 0, k, l)

            @pl.when(r != me)
            def _():
                pltpu.make_async_remote_copy(
                    src_ref=sbuf.at[r],
                    dst_ref=rbuf.at[me],
                    send_sem=a2a_send,
                    recv_sem=a2a_recv.at[mz],
                    device_id={"region": r},
                    device_id_type=pl.DeviceIdType.MESH,
                ).start()

            @pl.when(r == me)
            def _():
                pltpu.make_async_copy(sbuf.at[r], rbuf.at[me], a2a_recv.at[mz]).start()

    def send_plane(i, carry):
        z = lax.rem(mz + plane_offset(i), PLANES)
        pick_plane(z)
        copy_plane(z)
        return carry

    with jax.named_scope("send_columns"):
        pick_plane(lax.rem(mz + 1, PLANES))
        pl.semaphore_wait(barrier, REGIONS - 1 + len(beyond) + 1)
        copy_plane(lax.rem(mz + 1, PLANES))
        lax.fori_loop(1, PLANES, send_plane, 0)

    with jax.named_scope("tables"):
        ld_esrc.wait()
        ld_edst.wait()
        src = esrc_v[...]
        code_v[...] = (
            (src >> 9) * 256 + ((src >> 8) & 1) * 128 + (src & 127)
        ).astype(F32)
        jbit_v[...] = (src >> 7) & 1
        dstf_v[...] = edst_v[...].astype(F32)
        acc_v[...] = jnp.zeros((KCAT, EDGES), BF)
        tab_v[...] = jnp.zeros((2 * VPAD, 2 * SLOT), BF)
        ld_geom.wait()
        acc_v[VPAD : VPAD + GEO, :] = geom_v[...]
        ld_gw.wait()
        ld_ew.wait()
        wc_v[...] = jnp.zeros((KCAT, D), F32)
        wc_v[0:VARS, :] = gw_v[...].astype(F32)
        wc_v[VPAD : VPAD + GEO, :] = ew_v[...].astype(F32)
        wt_v[...] = wc_v[...].T.astype(BF)
        for e in range(EDGES // ETILE):
            row = lanes(dstf_v, e * (ETILE // 128), ETILE // 128).astype(BF)
            node_v[:, e * ETILE : (e + 1) * ETILE] = one_hot(row, NODES)
        ld_nb.wait()
        local = nb_v[...] - me * NODES + HALO
        local = jnp.where(local < 0, local + NODES * REGIONS, local)
        local = jnp.where(local >= NODES * REGIONS, local - NODES * REGIONS, local)
        for block in range(2 * NODES // 64):
            ids = lax.broadcasted_iota(jnp.int32, (64, NODES), 0) + block * 64
            total = jnp.zeros((64, NODES), F32)
            for j in range(K_NB):
                total = total + jnp.where(ids == local[j : j + 1, :], 1.0, 0.0)
            spot = slice(block * 64, (block + 1) * 64)
            count_t[spot, :] = total
        count_l[...] = count_t[HALO : HALO + NODES, :].T
        count_h[:, :HALO] = count_t[:HALO, :].T
        count_h[:, HALO:] = count_t[HALO + NODES :, :].T

    def gather_plane(i, carry):
        z = lax.rem(mz + PLANES - plane_offset(lax.rem(i + PLANES - 1, PLANES)), PLANES)
        window = rbuf.at[pl.ds(ROWS * z, ROWS)]
        pltpu.make_async_copy(window, window, a2a_recv.at[z]).wait()
        for k in range(ROWS):
            top, left = (k % 2) * VPAD, (k // 2) * SLOT
            tab_v[top : top + VARS, left : left + SLOT] = rbuf[ROWS * z + k]
        table = tab_v[...]
        base = (z * 256).astype(F32)
        for e in range(EDGES // ETILE):
            first = e * (ETILE // 128)
            cols = slice(e * ETILE, (e + 1) * ETILE)
            hot = one_hot((lanes(code_v, first, ETILE // 128) - base).astype(BF), 256)
            both = dot(table, hot)
            odd = lanes(jbit_v, first, ETILE // 128) == 1
            picked = jnp.where(odd, both[VPAD:, :], both[:VPAD, :]).astype(BF)
            acc_v[0:VPAD, cols] = acc_v[0:VPAD, cols] + picked
        return carry

    with jax.named_scope("gather_edges"):
        lax.fori_loop(0, PLANES, gather_plane, 0)

    with jax.named_scope("hidden"):
        for e in range(EDGES // ETILE):
            cols = slice(e * ETILE, (e + 1) * ETILE)
            x = dot(wt_v[...], acc_v[:, cols])
            half = (0.5 * x).astype(BF)
            hid_v[:, cols] = half + half * jnp.tanh(half)
        hidden_sum = dot_nt(node_v[...], hid_v[...])

    with jax.named_scope("encode"):
        ld_mw.wait()
        ld_mesh.wait()
        ld_eg.wait()
        ld_ag.wait()
        high = hidden_sum.astype(BF)
        rest = (hidden_sum - high.astype(F32)).astype(BF)
        aggregate = dot(high, mw_v[...]) + dot(rest, mw_v[...])
        encoded = mesh_v[...].astype(F32) + rms(aggregate, norm_eps) * eg_v[...]
        enc_v[...] = encoded
        nrm_v[...] = (rms(encoded, norm_eps) * ag_v[...]).astype(BF)

    step = HALO // HSPLIT
    for part in range(HSPLIT):
        for side, first, there, to in (
            (0, 0, HALO, region_prev),
            (1, NODES - HALO, 0, region_next),
        ):
            pltpu.make_async_remote_copy(
                src_ref=nrm_v.at[first + part * step : first + (part + 1) * step],
                dst_ref=halo_v.at[there + part * step : there + (part + 1) * step],
                send_sem=halo_send,
                recv_sem=halo_recv,
                device_id={"region": to},
                device_id_type=pl.DeviceIdType.MESH,
            ).start()
    halo_sent = pltpu.make_async_copy(nrm_v, nrm_v, halo_send)
    halo_got = pltpu.make_async_copy(halo_v, halo_v, halo_recv)

    with jax.named_scope("attention_local"):
        ld_qkv.wait()
        projected = dot(nrm_v[...], qkv_v[...])
        query = units(projected[:, :D])
        key = units(projected[:, D : 2 * D])
        value = projected[:, 2 * D :].astype(BF)
        rate = 1.0 / math.sqrt(HEAD)

        def mix(q, k, v, count):
            weight = (jnp.exp(dot_nt(q, k) * rate) * count).astype(BF)
            return dot(weight, with_ones(v))

        mixed = [
            mix(query[h], key[h], value[:, h * HEAD : (h + 1) * HEAD], count_l[...])
            for h in range(HEADS)
        ]

    other = pl.ds(pl.multiple_of((1 - core) * NODES, NODES), NODES)
    mine = pl.ds(pl.multiple_of(core * NODES, NODES), NODES)
    swaps = []

    def send_pieces(pair):
        swaps[pair].wait_recv()
        rows = slice(pair * 2 * HEAD, (pair + 1) * 2 * HEAD)
        total = p_v[rows, :] + rb1[rows, :].astype(F32)
        p_v[rows, :] = total
        sb2[rows, :] = total.astype(BF)
        for i, (dx, dy) in enumerate(AROUND):
            there = sixteen(pair, lax.rem(mx + dx, XS), lax.rem(my + dy, ROWS))
            pltpu.make_async_remote_copy(
                src_ref=sb2.at[there],
                dst_ref=rb2.at[i, pair * 16 : (pair + 1) * 16],
                send_sem=s2_send,
                recv_sem=s2_recv.at[pair],
                device_id=across(dx, dy),
                device_id_type=pl.DeviceIdType.MESH,
            ).start()

    with jax.named_scope("attention_halo"):
        halo_got.wait()
        ld_cot.wait()
        for pair in range(2):
            wide = 2 * HEAD
            beside = dot(halo_v[...], qkv_v[:, D + pair * wide : D + (pair + 1) * wide])
            value = dot(
                halo_v[...], qkv_v[:, 2 * D + pair * wide : 2 * D + (pair + 1) * wide]
            ).astype(BF)
            for h in range(2):
                head = 2 * pair + h
                cols = slice(h * HEAD, (h + 1) * HEAD)
                key = rms(beside[:, cols], head_eps).astype(BF)
                both = mixed[head] + mix(query[head], key, value[:, cols], count_h[...])
                att_v[:, head * HEAD : (head + 1) * HEAD] = both[:, :HEAD] / both[:, HEAD:]
            if pair == 1:
                send_pieces(0)
            rows = slice(pair * wide, (pair + 1) * wide)
            attt_v[rows, :] = att_v[:, rows].T.astype(BF)
            sb1[rows, :] = dot(attt_v[rows, :], cot_v[:, other]).astype(BF)
            swap = pltpu.make_async_remote_copy(
                src_ref=sb1.at[rows],
                dst_ref=rb1.at[rows],
                send_sem=s1_send.at[pair],
                recv_sem=s1_recv.at[pair],
                device_id={"noise": partner},
                device_id_type=pl.DeviceIdType.MESH,
            )
            swap.start()
            swaps.append(swap)
            p_v[rows, :] = dot(attt_v[rows, :], cot_v[:, mine])

    with jax.named_scope("reduce_xy"):
        send_pieces(1)

    with jax.named_scope("mesh_out"):
        ld_ow.wait()
        mout_v[...] = (enc_v[...] + dot(att_v[...].astype(BF), ow_v[...])).astype(BF)
        mesh_out = pltpu.make_async_copy(mout_v, mesh_out_hbm, out_sem.at[2 * XS])
        mesh_out.start()

    lots = [pl.ds(pair * 16, 16) for pair in range(2)]
    with jax.named_scope("reduce_z"):
        for pair, lot in enumerate(lots):
            window = rb2.at[:, lot]
            pltpu.make_async_copy(window, window, s2_recv.at[pair]).wait()
            total = p_v[sixteen(pair, mx, my), :]
            for i in range(len(AROUND)):
                total = total + rb2[i, lot].astype(F32)
            zbuf[mz, lot] = total.astype(BF)
            for d in (4, 3, 5, 2, 6, 1, 7):
                pltpu.make_async_remote_copy(
                    src_ref=zbuf.at[mz, lot],
                    dst_ref=zbuf.at[mz, lot],
                    send_sem=s3_send,
                    recv_sem=s3_recv.at[pair],
                    device_id={"region": lax.rem(me + ROWS * d, REGIONS)},
                    device_id_type=pl.DeviceIdType.MESH,
                ).start()

    with jax.named_scope("gather_xy"):
        for pair, lot in enumerate(lots):
            window = zbuf.at[0 : PLANES - 1, lot]
            pltpu.make_async_copy(window, window, s3_recv.at[pair]).wait()
            total = zbuf[0, lot].astype(F32)
            for z in range(1, PLANES):
                total = total + zbuf[z, lot].astype(F32)
            place = pl.ds(
                pl.multiple_of((mx * ROWS + my) * PIECE + pair * 16, 16), 16
            )
            fbuf[core, place, :] = total.astype(BF)
            for dx, dy in AROUND:
                pltpu.make_async_remote_copy(
                    src_ref=fbuf.at[core, place],
                    dst_ref=fbuf.at[core, place],
                    send_sem=g2_send,
                    recv_sem=g2_recv.at[dx],
                    device_id=across(dx, dy),
                    device_id_type=pl.DeviceIdType.MESH,
                ).start()

    with jax.named_scope("gather_core"):
        backs, outs = [], []
        for i, dx in enumerate((0, 1, 3, 2)):
            some = rb2.at[0 : ROWS - (dx == 0)]
            pltpu.make_async_copy(some, some, g2_recv.at[dx]).wait()
            rows = pl.ds(
                pl.multiple_of(lax.rem(mx + XS - dx, XS) * ROWS * PIECE, ROWS * PIECE),
                ROWS * PIECE,
            )
            back = pltpu.make_async_remote_copy(
                src_ref=fbuf.at[core, rows],
                dst_ref=fbuf.at[core, rows],
                send_sem=g1_send.at[i],
                recv_sem=g1_recv.at[i],
                device_id={"noise": partner},
                device_id_type=pl.DeviceIdType.MESH,
            )
            back.start()
            backs.append(back)
            out = pltpu.make_async_copy(
                fbuf.at[core, rows], grad_hbm.at[core, rows], out_sem.at[i]
            )
            out.start()
            outs.append((rows, out))
        for i in range(XS):
            backs[i].wait_recv()
            rows, out = outs[i]
            out = pltpu.make_async_copy(
                fbuf.at[1 - core, rows], grad_hbm.at[1 - core, rows], out_sem.at[XS + i]
            )
            out.start()
            outs.append((rows, out))

    sent = sbuf.at[0 : REGIONS - 1]
    pltpu.make_async_copy(sent, sent, a2a_send).wait()
    halo_sent.wait()
    for swap in swaps:
        swap.wait_send()
    pltpu.make_async_copy(rb2, rb2, s2_send).wait()
    seven = zbuf.at[0 : PLANES - 1]
    pltpu.make_async_copy(seven, seven, s3_send).wait()
    pltpu.make_async_copy(rb2, rb2, g2_send).wait()
    mesh_out.wait()
    for back in backs:
        back.wait_send()
    for _, out in outs:
        out.wait()


def widen(mesh_hbm, grad_hbm, mesh_out_hbm, grad_out_hbm, narrow, wide, mesh_v, in_sems, out_sems):
    parts = [(c, slice(i * 128, (i + 1) * 128)) for i in range(4) for c in range(2)]
    got = [
        pltpu.make_async_copy(grad_hbm.at[c, rows], narrow.at[c, rows], in_sems.at[i])
        for i, (c, rows) in enumerate(parts)
    ]
    mesh_got = pltpu.make_async_copy(mesh_hbm, mesh_v, in_sems.at[8])
    for copy in got:
        copy.start()
    mesh_got.start()
    sent = []
    for i, (c, rows) in enumerate(parts):
        got[i].wait()
        for q in range(4):
            for pair in range(2):
                first = rows.start + q * PIECE + pair * 16
                to = pair * NODES + (rows.start // PIECE + q) * 16
                wide[to : to + 16, c * NODES : (c + 1) * NODES] = narrow[
                    c, first : first + 16, :
                ].astype(F32)
        if c == 1:
            for pair in range(2):
                block = pl.ds(pair * NODES + rows.start // 2, 64)
                copy = pltpu.make_async_copy(
                    wide.at[block], grad_out_hbm.at[block], out_sems.at[i - 1 + pair]
                )
                copy.start()
                sent.append(copy)
    mesh_got.wait()
    copy = pltpu.make_async_copy(mesh_v, mesh_out_hbm.at[0], out_sems.at[8])
    copy.start()
    for copy in sent + [copy]:
        copy.wait()


def body(
    target_state,
    noise_field,
    level_index,
    send_rows,
    edge_src,
    edge_dst,
    edge_geom,
    mesh_init,
    neighbours,
    grid_weight,
    edge_weight,
    message_weight,
    enc_gain,
    att_gain,
    qkv_weight,
    out_weight,
    cotangent,
):
    operands = (
        level_index.reshape(1, 1),
        send_rows,
        edge_src.reshape(EDGES // 128, 128),
        edge_dst.reshape(EDGES // 128, 128),
        neighbours.T,
        target_state,
        noise_field,
        edge_geom,
        mesh_init,
        grid_weight,
        edge_weight,
        message_weight,
        enc_gain.reshape(1, D),
        att_gain.reshape(1, D),
        qkv_weight,
        out_weight,
        cotangent,
    )
    vmem = pltpu.VMEM
    dma = pltpu.SemaphoreType.DMA
    i32 = jnp.int32
    scratch = [
        vmem((REGIONS, SLOT), i32),
        vmem((EDGES // 128, 128), i32),
        vmem((EDGES // 128, 128), i32),
        vmem((K_NB, NODES), i32),
        vmem((VARS, GRID), BF),
        vmem((VARS, GRID), BF),
        vmem((GEO, EDGES), BF),
        vmem((NODES, D), BF),
        vmem((VARS, D), BF),
        vmem((GEO, D), BF),
        vmem((D, D), BF),
        vmem((1, D), F32),
        vmem((1, D), F32),
        vmem((D, 3 * D), BF),
        vmem((D, D), BF),
        vmem((NODES, D), BF),
        dma((16,)),
        vmem((2 * VPAD, HALF), BF),
        vmem((REGIONS, VARS, SLOT), BF),
        vmem((REGIONS, VARS, SLOT), BF),
        vmem((EDGES // 128, 128), F32),
        vmem((EDGES // 128, 128), i32),
        vmem((EDGES // 128, 128), F32),
        vmem((KCAT, D), F32),
        vmem((D, KCAT), BF),
        vmem((2 * VPAD, 2 * SLOT), BF),
        vmem((KCAT, EDGES), BF),
        vmem((NODES, EDGES), BF),
        vmem((D, EDGES), BF),
        vmem((2 * NODES, NODES), F32),
        vmem((NODES, NODES), F32),
        vmem((NODES, NODES), F32),
        vmem((NODES, D), F32),
        vmem((NODES, D), BF),
        vmem((2 * HALO, D), BF),
        vmem((NODES, D), F32),
        vmem((D, NODES), BF),
        dma,
        dma((PLANES,)),
        dma,
        dma,
        vmem((D, NODES), F32),
        vmem((D, NODES), BF),
        vmem((D, NODES), BF),
        vmem((D, NODES), BF),
        vmem((len(AROUND), PIECE, NODES), BF),
        vmem((PLANES, PIECE, NODES), BF),
        vmem((2, D, NODES), BF),
        vmem((NODES, D), BF),
        dma((2,)),
        dma((2,)),
    ] + [dma, dma((2,)), dma, dma((2,)), dma] + [dma((XS,))] * 3 + [dma((2 * XS + 1,))]
    mesh_out, grad = pl.pallas_call(
        kernel,
        out_shape=(
            jax.ShapeDtypeStruct((NODES, D), BF),
            jax.ShapeDtypeStruct((2, D, NODES), BF),
        ),
        in_specs=[pl.BlockSpec(memory_space=pltpu.VMEM)]
        + [pl.BlockSpec(memory_space=pl.ANY)] * (len(operands) - 1),
        out_specs=[pl.BlockSpec(memory_space=pl.ANY)] * 2,
        scratch_shapes=scratch,
        compiler_params=pltpu.CompilerParams(
            collective_id=0, has_side_effects=True, vmem_limit_bytes=60 * 1024 * 1024
        ),
        cost_estimate=pl.CostEstimate(
            flops=12_000_000_000, bytes_accessed=6_000_000, transcendentals=3_000_000
        ),
    )(*operands)
    mesh_out, grad = pl.pallas_call(
        widen,
        out_shape=(
            jax.ShapeDtypeStruct((1, NODES, D), BF),
            jax.ShapeDtypeStruct((D, D), F32),
        ),
        in_specs=[pl.BlockSpec(memory_space=pl.ANY)] * 2,
        out_specs=[pl.BlockSpec(memory_space=pl.ANY)] * 2,
        scratch_shapes=[
            vmem((2, D, NODES), BF),
            vmem((D, D), F32),
            vmem((NODES, D), BF),
            dma((9,)),
            dma((9,)),
        ],
    )(mesh_out, grad)
    return mesh_out, grad


def solution(mesh):
    in_specs = (
        P(None, "region"),
        P("noise", None, "region"),
        P("noise"),
        P("region", None, None),
        P("region"),
        P("region"),
        P(None, "region"),
        P("region", None),
        P("region", None),
        P(),
        P(),
        P(),
        P(),
        P(),
        P(),
        P(),
        P("noise", "region", None),
    )
    out_specs = (P("noise", "region", None), P())
    return jax.shard_map(body, mesh=mesh, in_specs=in_specs, out_specs=out_specs, check_vma=False)
```

```python
import math

import jax
import jax.numpy as jnp
from jax import lax
from jax.experimental import pallas as pl
from jax.experimental.pallas import tpu as pltpu
from jax.sharding import PartitionSpec as P

BF = jnp.bfloat16
F32 = jnp.float32

D = 512
HEADS = 4
HEAD = 128
VARS = 84
VPAD = 96
GEO = 4
PLAN = 20
K_NB = 32
HALO = 128
NODES = 256
GRID = 2048
EDGES = 4096
SLOT = 128
REGIONS = 32
PLANES = 8
ROWS = 4
XS = 4
ETILE = 512
HSPLIT = 1
PIECE = 32
HALF = GRID // 2
KCAT = 128

sigma_max = 80.0
sigma_min = 0.03
plan_rho = 7.0
norm_eps = 1e-05
head_eps = 1e-06

UP_ROOT = sigma_max ** (1.0 / plan_rho)
LOW_ROOT = sigma_min ** (1.0 / plan_rho)

AROUND = sorted(
    [(dx, dy) for dx in range(XS) for dy in range(ROWS) if dx or dy],
    key=lambda d: (-min(d[0], XS - d[0]) - min(d[1], ROWS - d[1]), d),
)

COLUMN = sorted(
    [(dy, dz) for dy in range(ROWS) for dz in range(PLANES) if dy or dz],
    key=lambda d: (-min(d[0], ROWS - d[0]) - min(d[1], PLANES - d[1]), d),
)

NT = (((1,), (1,)), ((), ()))


def dot(a, b):
    return jnp.dot(a, b, preferred_element_type=F32)


def dot_nt(a, b):
    return lax.dot_general(a, b, NT, preferred_element_type=F32)


def one_hot(code_row, rows):
    n = code_row.shape[1]
    ids = lax.broadcasted_iota(jnp.int32, (rows, n), 0).astype(F32).astype(BF)
    want = jnp.broadcast_to(code_row, (rows, n))
    return jnp.where(ids == want, jnp.ones((), BF), jnp.zeros((), BF))


def lanes(ref, first, count):
    return jnp.concatenate([ref[pl.ds(first + k, 1), :] for k in range(count)], axis=1)


def rms(values, epsilon):
    return values * lax.rsqrt(jnp.mean(values * values, axis=-1, keepdims=True) + epsilon)


def units(projected):
    return [
        rms(projected[:, h * HEAD : (h + 1) * HEAD], head_eps).astype(BF) for h in range(HEADS)
    ]


def with_ones(values):
    return jnp.concatenate([values, jnp.ones(values.shape, BF)], axis=1)


def plane_offset(i):
    half = lax.div(i, 2) + 1
    return jnp.where(
        i == PLANES - 1, 0, jnp.where(lax.rem(i, 2) == 0, half, PLANES - half)
    )


def kernel(
    level_ref,
    send_hbm,
    esrc_hbm,
    edst_hbm,
    nb_hbm,
    target_hbm,
    noise_hbm,
    geom_hbm,
    mesh_hbm,
    gw_hbm,
    ew_hbm,
    mw_hbm,
    eg_hbm,
    ag_hbm,
    qkv_hbm,
    ow_hbm,
    cot_hbm,
    mesh_out_hbm,
    grad_hbm,
    send_v,
    esrc_v,
    edst_v,
    nb_v,
    target_v,
    noise_v,
    geom_v,
    mesh_v,
    gw_v,
    ew_v,
    mw_v,
    eg_v,
    ag_v,
    qkv_v,
    ow_v,
    cot_v,
    in_sem,
    g_v,
    sbuf,
    rbuf,
    code_v,
    jbit_v,
    dstf_v,
    wc_v,
    wt_v,
    tab_v,
    acc_v,
    node_v,
    hid_v,
    count_t,
    count_l,
    count_h,
    enc_v,
    nrm_v,
    halo_v,
    att_v,
    attt_v,
    a2a_send,
    a2a_recv,
    halo_send,
    halo_recv,
    p_v,
    sb1,
    rb1,
    sb2,
    rb2,
    zbuf,
    fbuf,
    mout_v,
    s1_send,
    s1_recv,
    s2_send,
    s2_recv,
    s3_send,
    s3_recv,
    g2_send,
    g2_recv,
    g1_send,
    g1_recv,
    out_sem,
):
    noise = lax.axis_index("noise")
    me = lax.axis_index("region")
    core = lax.rem(noise, 2)
    mx = lax.div(noise, 2)
    mz = lax.div(me, ROWS)
    my = lax.rem(me, ROWS)
    partner = noise + 1 - 2 * core
    region_next = lax.rem(me + 1, REGIONS)
    region_prev = lax.rem(me + REGIONS - 1, REGIONS)

    def across(dx, dy):
        return {
            "noise": lax.rem(mx + dx, XS) * 2 + core,
            "region": mz * ROWS + lax.rem(my + dy, ROWS),
        }

    def region_at(dy, dz):
        return lax.rem(mz + dz, PLANES) * ROWS + lax.rem(my + dy, ROWS)

    def sixteen(pair, x, y):
        return pl.ds(pl.multiple_of(pair * NODES + (x * ROWS + y) * 16, 16), 16)

    def piece(x, y):
        return pl.ds(pl.multiple_of((x * ROWS + y) * PIECE, PIECE), PIECE)

    pairs = [
        (noise_hbm.at[0], noise_v),
        (target_hbm, target_v),
        (send_hbm.at[0], send_v),
        (esrc_hbm, esrc_v),
        (edst_hbm, edst_v),
        (nb_hbm, nb_v),
        (geom_hbm, geom_v),
        (gw_hbm, gw_v),
        (ew_hbm, ew_v),
        (mw_hbm, mw_v),
        (mesh_hbm, mesh_v),
        (eg_hbm, eg_v),
        (ag_hbm, ag_v),
        (qkv_hbm, qkv_v),
        (cot_hbm.at[0], cot_v),
        (ow_hbm, ow_v),
    ]
    loads = [pltpu.make_async_copy(s, d, in_sem.at[i]) for i, (s, d) in enumerate(pairs)]
    (
        ld_noise,
        ld_target,
        ld_send,
        ld_esrc,
        ld_edst,
        ld_nb,
        ld_geom,
        ld_gw,
        ld_ew,
        ld_mw,
        ld_mesh,
        ld_eg,
        ld_ag,
        ld_qkv,
        ld_cot,
        ld_ow,
    ) = loads
    for load in loads[:3]:
        load.start()

    barrier = pltpu.get_barrier_semaphore()

    def tell(device):
        pl.semaphore_signal(
            barrier, inc=1, device_id=device, device_id_type=pl.DeviceIdType.MESH
        )

    for dy, dz in COLUMN:
        tell({"region": region_at(dy, dz)})
    beyond = [(dx, dy) for dx, dy in AROUND if dx]
    for dx, dy in beyond:
        tell(across(dx, dy))
    tell({"noise": partner})
    for load in loads[3:]:
        load.start()

    g_v[80:96, :] = jnp.zeros((16, HALF), BF)
    g_v[176:192, :] = jnp.zeros((16, HALF), BF)
    level = jnp.broadcast_to(level_ref[...], (1, HALF)).astype(F32) * (1.0 / (PLAN - 1))
    root = UP_ROOT + level * (LOW_ROOT - UP_ROOT)
    root2 = root * root
    sigma = root2 * root2 * root2 * root
    scale = lax.rsqrt(1.0 + sigma * sigma)
    ld_noise.wait()
    ld_target.wait()
    for part in range(2):
        cols = slice(part * HALF, (part + 1) * HALF)
        noised = (
            target_v[:, cols].astype(F32) + sigma * noise_v[:, cols].astype(F32)
        ) * scale
        g_v[part * VPAD : part * VPAD + VARS, :] = noised.astype(BF)
    ld_send.wait()
    def pick_plane(z):
        idx = lanes(send_v, ROWS * z, ROWS)
        upper = idx >= HALF
        low = jnp.where(upper, idx - HALF, idx).astype(F32)
        hot = jnp.concatenate(
            [one_hot((low - 256.0 * k).astype(BF), 256) for k in range(HALF // 256)], axis=0
        )
        both = dot(g_v[...], hot)
        picked = jnp.where(upper, both[VPAD:, :], both[:VPAD, :]).astype(BF)
        for k in range(ROWS):
            sbuf[ROWS * z + k] = picked[:VARS, k * SLOT : (k + 1) * SLOT]

    def copy_plane(z):
        for k, l in ((0, 3), (3, 0), (1, 2), (2, 1)):
            r = ROWS * z + jnp.where(lax.rem(z, 2) == 0, k, l)

            @pl.when(r != me)
            def _():
                pltpu.make_async_remote_copy(
                    src_ref=sbuf.at[r],
                    dst_ref=rbuf.at[me],
                    send_sem=a2a_send,
                    recv_sem=a2a_recv.at[mz],
                    device_id={"region": r},
                    device_id_type=pl.DeviceIdType.MESH,
                ).start()

            @pl.when(r == me)
            def _():
                pltpu.make_async_copy(sbuf.at[r], rbuf.at[me], a2a_recv.at[mz]).start()

    def send_plane(i, carry):
        z = lax.rem(mz + plane_offset(i), PLANES)
        pick_plane(z)

        @pl.when(core == 0)
        def _():
            copy_plane(z)

        return carry

    def late_plane(i, carry):
        copy_plane(lax.rem(mz + plane_offset(i), PLANES))
        return carry

    with jax.named_scope("send_columns"):
        pick_plane(lax.rem(mz + 1, PLANES))
        pl.semaphore_wait(barrier, REGIONS - 1 + len(beyond) + 1)

        @pl.when(core == 0)
        def _():
            copy_plane(lax.rem(mz + 1, PLANES))

        lax.fori_loop(1, PLANES, send_plane, 0)

        @pl.when(core == 1)
        def _():
            lax.fori_loop(0, PLANES, late_plane, 0)

    with jax.named_scope("tables"):
        ld_esrc.wait()
        ld_edst.wait()
        src = esrc_v[...]
        code_v[...] = (
            (src >> 9) * 256 + ((src >> 8) & 1) * 128 + (src & 127)
        ).astype(F32)
        jbit_v[...] = (src >> 7) & 1
        dstf_v[...] = edst_v[...].astype(F32)
        acc_v[...] = jnp.zeros((KCAT, EDGES), BF)
        tab_v[...] = jnp.zeros((2 * VPAD, 2 * SLOT), BF)
        ld_geom.wait()
        acc_v[VPAD : VPAD + GEO, :] = geom_v[...]
        ld_gw.wait()
        ld_ew.wait()
        wc_v[...] = jnp.zeros((KCAT, D), F32)
        wc_v[0:VARS, :] = gw_v[...].astype(F32)
        wc_v[VPAD : VPAD + GEO, :] = ew_v[...].astype(F32)
        wt_v[...] = wc_v[...].T.astype(BF)
        for e in range(EDGES // ETILE):
            row = lanes(dstf_v, e * (ETILE // 128), ETILE // 128).astype(BF)
            node_v[:, e * ETILE : (e + 1) * ETILE] = one_hot(row, NODES)
        ld_nb.wait()
        local = nb_v[...] - me * NODES + HALO
        local = jnp.where(local < 0, local + NODES * REGIONS, local)
        local = jnp.where(local >= NODES * REGIONS, local - NODES * REGIONS, local)
        for block in range(2 * NODES // 64):
            ids = lax.broadcasted_iota(jnp.int32, (64, NODES), 0) + block * 64
            total = jnp.zeros((64, NODES), F32)
            for j in range(K_NB):
                total = total + jnp.where(ids == local[j : j + 1, :], 1.0, 0.0)
            spot = slice(block * 64, (block + 1) * 64)
            count_t[spot, :] = total
        count_l[...] = count_t[HALO : HALO + NODES, :].T
        count_h[:, :HALO] = count_t[:HALO, :].T
        count_h[:, HALO:] = count_t[HALO + NODES :, :].T

    def gather_plane(i, carry):
        z = lax.rem(mz + PLANES - plane_offset(lax.rem(i + PLANES - 1, PLANES)), PLANES)
        window = rbuf.at[pl.ds(ROWS * z, ROWS)]
        pltpu.make_async_copy(window, window, a2a_recv.at[z]).wait()
        for k in range(ROWS):
            top, left = (k % 2) * VPAD, (k // 2) * SLOT
            tab_v[top : top + VARS, left : left + SLOT] = rbuf[ROWS * z + k]
        table = tab_v[...]
        base = (z * 256).astype(F32)
        for e in range(EDGES // ETILE):
            first = e * (ETILE // 128)
            cols = slice(e * ETILE, (e + 1) * ETILE)
            hot = one_hot((lanes(code_v, first, ETILE // 128) - base).astype(BF), 256)
            both = dot(table, hot)
            odd = lanes(jbit_v, first, ETILE // 128) == 1
            picked = jnp.where(odd, both[VPAD:, :], both[:VPAD, :]).astype(BF)
            acc_v[0:VPAD, cols] = acc_v[0:VPAD, cols] + picked
        return carry

    with jax.named_scope("gather_edges"):
        lax.fori_loop(0, PLANES, gather_plane, 0)

    with jax.named_scope("hidden"):
        for e in range(EDGES // ETILE):
            cols = slice(e * ETILE, (e + 1) * ETILE)
            x = dot(wt_v[...], acc_v[:, cols])
            half = (0.5 * x).astype(BF)
            hid_v[:, cols] = half + half * jnp.tanh(half)
        hidden_sum = dot_nt(node_v[...], hid_v[...])

    with jax.named_scope("encode"):
        ld_mw.wait()
        ld_mesh.wait()
        ld_eg.wait()
        ld_ag.wait()
        high = hidden_sum.astype(BF)
        rest = (hidden_sum - high.astype(F32)).astype(BF)
        aggregate = dot(high, mw_v[...]) + dot(rest, mw_v[...])
        encoded = mesh_v[...].astype(F32) + rms(aggregate, norm_eps) * eg_v[...]
        enc_v[...] = encoded
        nrm_v[...] = (rms(encoded, norm_eps) * ag_v[...]).astype(BF)

    step = HALO // HSPLIT
    for part in range(HSPLIT):
        for side, first, there, to in (
            (0, 0, HALO, region_prev),
            (1, NODES - HALO, 0, region_next),
        ):
            pltpu.make_async_remote_copy(
                src_ref=nrm_v.at[first + part * step : first + (part + 1) * step],
                dst_ref=halo_v.at[there + part * step : there + (part + 1) * step],
                send_sem=halo_send,
                recv_sem=halo_recv,
                device_id={"region": to},
                device_id_type=pl.DeviceIdType.MESH,
            ).start()
    halo_sent = pltpu.make_async_copy(nrm_v, nrm_v, halo_send)
    halo_got = pltpu.make_async_copy(halo_v, halo_v, halo_recv)

    with jax.named_scope("attention_local"):
        ld_qkv.wait()
        projected = dot(nrm_v[...], qkv_v[...])
        query = units(projected[:, :D])
        key = units(projected[:, D : 2 * D])
        value = projected[:, 2 * D :].astype(BF)
        rate = 1.0 / math.sqrt(HEAD)

        def mix(q, k, v, count):
            weight = (jnp.exp(dot_nt(q, k) * rate) * count).astype(BF)
            return dot(weight, with_ones(v))

        mixed = [
            mix(query[h], key[h], value[:, h * HEAD : (h + 1) * HEAD], count_l[...])
            for h in range(HEADS)
        ]

    other = pl.ds(pl.multiple_of((1 - core) * NODES, NODES), NODES)
    mine = pl.ds(pl.multiple_of(core * NODES, NODES), NODES)
    swaps = []

    def send_pieces(pair):
        swaps[pair].wait_recv()
        rows = slice(pair * 2 * HEAD, (pair + 1) * 2 * HEAD)
        total = p_v[rows, :] + rb1[rows, :].astype(F32)
        p_v[rows, :] = total
        sb2[rows, :] = total.astype(BF)
        for i, (dx, dy) in enumerate(AROUND):
            there = sixteen(pair, lax.rem(mx + dx, XS), lax.rem(my + dy, ROWS))
            pltpu.make_async_remote_copy(
                src_ref=sb2.at[there],
                dst_ref=rb2.at[i, pair * 16 : (pair + 1) * 16],
                send_sem=s2_send,
                recv_sem=s2_recv.at[pair],
                device_id=across(dx, dy),
                device_id_type=pl.DeviceIdType.MESH,
            ).start()

    with jax.named_scope("attention_halo"):
        halo_got.wait()
        ld_cot.wait()
        for pair in range(2):
            wide = 2 * HEAD
            beside = dot(halo_v[...], qkv_v[:, D + pair * wide : D + (pair + 1) * wide])
            value = dot(
                halo_v[...], qkv_v[:, 2 * D + pair * wide : 2 * D + (pair + 1) * wide]
            ).astype(BF)
            for h in range(2):
                head = 2 * pair + h
                cols = slice(h * HEAD, (h + 1) * HEAD)
                key = rms(beside[:, cols], head_eps).astype(BF)
                both = mixed[head] + mix(query[head], key, value[:, cols], count_h[...])
                att_v[:, head * HEAD : (head + 1) * HEAD] = both[:, :HEAD] / both[:, HEAD:]
            if pair == 1:
                send_pieces(0)
            rows = slice(pair * wide, (pair + 1) * wide)
            attt_v[rows, :] = att_v[:, rows].T.astype(BF)
            sb1[rows, :] = dot(attt_v[rows, :], cot_v[:, other]).astype(BF)
            swap = pltpu.make_async_remote_copy(
                src_ref=sb1.at[rows],
                dst_ref=rb1.at[rows],
                send_sem=s1_send.at[pair],
                recv_sem=s1_recv.at[pair],
                device_id={"noise": partner},
                device_id_type=pl.DeviceIdType.MESH,
            )
            swap.start()
            swaps.append(swap)
            p_v[rows, :] = dot(attt_v[rows, :], cot_v[:, mine])

    with jax.named_scope("reduce_xy"):
        send_pieces(1)

    with jax.named_scope("mesh_out"):
        ld_ow.wait()
        mout_v[...] = (enc_v[...] + dot(att_v[...].astype(BF), ow_v[...])).astype(BF)
        mesh_out = pltpu.make_async_copy(mout_v, mesh_out_hbm, out_sem.at[2 * XS])
        mesh_out.start()

    lots = [pl.ds(pair * 16, 16) for pair in range(2)]
    with jax.named_scope("reduce_z"):
        for pair, lot in enumerate(lots):
            window = rb2.at[:, lot]
            pltpu.make_async_copy(window, window, s2_recv.at[pair]).wait()
            total = p_v[sixteen(pair, mx, my), :]
            for i in range(len(AROUND)):
                total = total + rb2[i, lot].astype(F32)
            zbuf[mz, lot] = total.astype(BF)
            for d in (4, 3, 5, 2, 6, 1, 7):
                pltpu.make_async_remote_copy(
                    src_ref=zbuf.at[mz, lot],
                    dst_ref=zbuf.at[mz, lot],
                    send_sem=s3_send,
                    recv_sem=s3_recv.at[pair],
                    device_id={"region": lax.rem(me + ROWS * d, REGIONS)},
                    device_id_type=pl.DeviceIdType.MESH,
                ).start()

    with jax.named_scope("gather_xy"):
        for pair, lot in enumerate(lots):
            window = zbuf.at[0 : PLANES - 1, lot]
            pltpu.make_async_copy(window, window, s3_recv.at[pair]).wait()
            total = zbuf[0, lot].astype(F32)
            for z in range(1, PLANES):
                total = total + zbuf[z, lot].astype(F32)
            place = pl.ds(
                pl.multiple_of((mx * ROWS + my) * PIECE + pair * 16, 16), 16
            )
            fbuf[core, place, :] = total.astype(BF)
            for dx, dy in AROUND:
                pltpu.make_async_remote_copy(
                    src_ref=fbuf.at[core, place],
                    dst_ref=fbuf.at[core, place],
                    send_sem=g2_send,
                    recv_sem=g2_recv.at[dx],
                    device_id=across(dx, dy),
                    device_id_type=pl.DeviceIdType.MESH,
                ).start()

    with jax.named_scope("gather_core"):
        backs, outs = [], []
        for i, dx in enumerate((0, 1, 3, 2)):
            some = rb2.at[0 : ROWS - (dx == 0)]
            pltpu.make_async_copy(some, some, g2_recv.at[dx]).wait()
            rows = pl.ds(
                pl.multiple_of(lax.rem(mx + XS - dx, XS) * ROWS * PIECE, ROWS * PIECE),
                ROWS * PIECE,
            )
            back = pltpu.make_async_remote_copy(
                src_ref=fbuf.at[core, rows],
                dst_ref=fbuf.at[core, rows],
                send_sem=g1_send.at[i],
                recv_sem=g1_recv.at[i],
                device_id={"noise": partner},
                device_id_type=pl.DeviceIdType.MESH,
            )
            back.start()
            backs.append(back)
            out = pltpu.make_async_copy(
                fbuf.at[core, rows], grad_hbm.at[core, rows], out_sem.at[i]
            )
            out.start()
            outs.append((rows, out))
        for i in range(XS):
            backs[i].wait_recv()
            rows, out = outs[i]
            out = pltpu.make_async_copy(
                fbuf.at[1 - core, rows], grad_hbm.at[1 - core, rows], out_sem.at[XS + i]
            )
            out.start()
            outs.append((rows, out))

    sent = sbuf.at[0 : REGIONS - 1]
    pltpu.make_async_copy(sent, sent, a2a_send).wait()
    halo_sent.wait()
    for swap in swaps:
        swap.wait_send()
    pltpu.make_async_copy(rb2, rb2, s2_send).wait()
    seven = zbuf.at[0 : PLANES - 1]
    pltpu.make_async_copy(seven, seven, s3_send).wait()
    pltpu.make_async_copy(rb2, rb2, g2_send).wait()
    mesh_out.wait()
    for back in backs:
        back.wait_send()
    for _, out in outs:
        out.wait()


def widen(mesh_hbm, grad_hbm, mesh_out_hbm, grad_out_hbm, narrow, wide, mesh_v, in_sems, out_sems):
    parts = [(c, slice(i * 128, (i + 1) * 128)) for i in range(4) for c in range(2)]
    got = [
        pltpu.make_async_copy(grad_hbm.at[c, rows], narrow.at[c, rows], in_sems.at[i])
        for i, (c, rows) in enumerate(parts)
    ]
    mesh_got = pltpu.make_async_copy(mesh_hbm, mesh_v, in_sems.at[8])
    for copy in got:
        copy.start()
    mesh_got.start()
    sent = []
    for i, (c, rows) in enumerate(parts):
        got[i].wait()
        for q in range(4):
            for pair in range(2):
                first = rows.start + q * PIECE + pair * 16
                to = pair * NODES + (rows.start // PIECE + q) * 16
                wide[to : to + 16, c * NODES : (c + 1) * NODES] = narrow[
                    c, first : first + 16, :
                ].astype(F32)
        if c == 1:
            for pair in range(2):
                block = pl.ds(pair * NODES + rows.start // 2, 64)
                copy = pltpu.make_async_copy(
                    wide.at[block], grad_out_hbm.at[block], out_sems.at[i - 1 + pair]
                )
                copy.start()
                sent.append(copy)
    mesh_got.wait()
    copy = pltpu.make_async_copy(mesh_v, mesh_out_hbm.at[0], out_sems.at[8])
    copy.start()
    for copy in sent + [copy]:
        copy.wait()


def body(
    target_state,
    noise_field,
    level_index,
    send_rows,
    edge_src,
    edge_dst,
    edge_geom,
    mesh_init,
    neighbours,
    grid_weight,
    edge_weight,
    message_weight,
    enc_gain,
    att_gain,
    qkv_weight,
    out_weight,
    cotangent,
):
    operands = (
        level_index.reshape(1, 1),
        send_rows,
        edge_src.reshape(EDGES // 128, 128),
        edge_dst.reshape(EDGES // 128, 128),
        neighbours.T,
        target_state,
        noise_field,
        edge_geom,
        mesh_init,
        grid_weight,
        edge_weight,
        message_weight,
        enc_gain.reshape(1, D),
        att_gain.reshape(1, D),
        qkv_weight,
        out_weight,
        cotangent,
    )
    vmem = pltpu.VMEM
    dma = pltpu.SemaphoreType.DMA
    i32 = jnp.int32
    scratch = [
        vmem((REGIONS, SLOT), i32),
        vmem((EDGES // 128, 128), i32),
        vmem((EDGES // 128, 128), i32),
        vmem((K_NB, NODES), i32),
        vmem((VARS, GRID), BF),
        vmem((VARS, GRID), BF),
        vmem((GEO, EDGES), BF),
        vmem((NODES, D), BF),
        vmem((VARS, D), BF),
        vmem((GEO, D), BF),
        vmem((D, D), BF),
        vmem((1, D), F32),
        vmem((1, D), F32),
        vmem((D, 3 * D), BF),
        vmem((D, D), BF),
        vmem((NODES, D), BF),
        dma((16,)),
        vmem((2 * VPAD, HALF), BF),
        vmem((REGIONS, VARS, SLOT), BF),
        vmem((REGIONS, VARS, SLOT), BF),
        vmem((EDGES // 128, 128), F32),
        vmem((EDGES // 128, 128), i32),
        vmem((EDGES // 128, 128), F32),
        vmem((KCAT, D), F32),
        vmem((D, KCAT), BF),
        vmem((2 * VPAD, 2 * SLOT), BF),
        vmem((KCAT, EDGES), BF),
        vmem((NODES, EDGES), BF),
        vmem((D, EDGES), BF),
        vmem((2 * NODES, NODES), F32),
        vmem((NODES, NODES), F32),
        vmem((NODES, NODES), F32),
        vmem((NODES, D), F32),
        vmem((NODES, D), BF),
        vmem((2 * HALO, D), BF),
        vmem((NODES, D), F32),
        vmem((D, NODES), BF),
        dma,
        dma((PLANES,)),
        dma,
        dma,
        vmem((D, NODES), F32),
        vmem((D, NODES), BF),
        vmem((D, NODES), BF),
        vmem((D, NODES), BF),
        vmem((len(AROUND), PIECE, NODES), BF),
        vmem((PLANES, PIECE, NODES), BF),
        vmem((2, D, NODES), BF),
        vmem((NODES, D), BF),
        dma((2,)),
        dma((2,)),
    ] + [dma, dma((2,)), dma, dma((2,)), dma] + [dma((XS,))] * 3 + [dma((2 * XS + 1,))]
    mesh_out, grad = pl.pallas_call(
        kernel,
        out_shape=(
            jax.ShapeDtypeStruct((NODES, D), BF),
            jax.ShapeDtypeStruct((2, D, NODES), BF),
        ),
        in_specs=[pl.BlockSpec(memory_space=pltpu.VMEM)]
        + [pl.BlockSpec(memory_space=pl.ANY)] * (len(operands) - 1),
        out_specs=[pl.BlockSpec(memory_space=pl.ANY)] * 2,
        scratch_shapes=scratch,
        compiler_params=pltpu.CompilerParams(
            collective_id=0, has_side_effects=True, vmem_limit_bytes=60 * 1024 * 1024
        ),
        cost_estimate=pl.CostEstimate(
            flops=12_000_000_000, bytes_accessed=6_000_000, transcendentals=3_000_000
        ),
    )(*operands)
    mesh_out, grad = pl.pallas_call(
        widen,
        out_shape=(
            jax.ShapeDtypeStruct((1, NODES, D), BF),
            jax.ShapeDtypeStruct((D, D), F32),
        ),
        in_specs=[pl.BlockSpec(memory_space=pl.ANY)] * 2,
        out_specs=[pl.BlockSpec(memory_space=pl.ANY)] * 2,
        scratch_shapes=[
            vmem((2, D, NODES), BF),
            vmem((D, D), F32),
            vmem((NODES, D), BF),
            dma((9,)),
            dma((9,)),
        ],
    )(mesh_out, grad)
    return mesh_out, grad


def solution(mesh):
    in_specs = (
        P(None, "region"),
        P("noise", None, "region"),
        P("noise"),
        P("region", None, None),
        P("region"),
        P("region"),
        P(None, "region"),
        P("region", None),
        P("region", None),
        P(),
        P(),
        P(),
        P(),
        P(),
        P(),
        P(),
        P("noise", "region", None),
    )
    out_specs = (P("noise", "region", None), P())
    return jax.shard_map(body, mesh=mesh, in_specs=in_specs, out_specs=out_specs, check_vma=False)
```
